32 devices in a mesh: traj: 2 (over y), ctx: 8 (over z, x), head: 2 (over core).
Axes of the slice: x: 2, y: 2, z: 4, core: 2. Of those that a mesh axis runs over, the one named last changes fastest.
Arguments:
- features: bfloat16 [4096, 2048], P(('traj', 'ctx'), 'head'), parts along dimension 0, may hold values from -6 to 6
- b_input: bfloat16 [4096, 128], P(('traj', 'ctx')), parts along dimension 0, may hold values from -1.5 to 1.5
- c_input: bfloat16 [4096, 128], P(('traj', 'ctx')), parts along dimension 0, may hold values from -1.5 to 1.5
- step_input: float32 [64, 4096], P('head', ('traj', 'ctx')), parts along dimension 1, may hold values from -5.5 to 18.78016
- decay_log: float32 [64], P('head')
- skip_gain: float32 [64], P('head'), may hold values from 0.5 to 2
- norm_gain: float32 [2048], P('head'), may hold values from 0.25 to 1.75
- value_weight: float32 [2048], P('head'), may hold values from -0.125 to 0.125
- rewards: float32 [4096], P(('traj', 'ctx')), parts along dimension 0, may hold values from -0.3 to 0.3
- reward_keep_mask: int32 [4096], P(('traj', 'ctx')), parts along dimension 0, may hold values 0 or 1
- episode_end: int32 [4096], P(('traj', 'ctx')), parts along dimension 0, may hold values from 0 to 1
Outputs:
- values: float32 [4096], P(('traj', 'ctx')), parts along dimension 0
- advantages: float32 [4096], P(('traj', 'ctx')), parts along dimension 0
The draws below stay inside these ranges and needn't reach their ends.
There are 2 independent parts, one for each index of `traj`. The reference program is written for one: setup_inputs(seed, part) draws one part's arguments, and reference() takes and returns one part's arrays. A program takes and returns all parts, laid end to end along the dimension named above; an argument that names none is the same for every part. Nothing has to cross between parts.
All inputs are finite; a program needn't handle non-finite values. No bound on the sum of `reward_keep_mask` on one device may be relied on, other than what follows from the above.
Results may differ from the reference program's by a relative error of at most 0.00037.
Values sent between devices are 32-bit elements; how exact they have to be, the bound alone decides.
No kernel may reach another device: no remote copies, remote signals or barrier semaphores. Data moves between devices by JAX's collectives and lax.ppermute only.
A program may use at most 192 MiB of HBM per device.

```python
import jax
import jax.numpy as jnp
from jax import lax

HEADS = 64
HEAD_DIM = 32
STATE = 128
SPAN = 256
TOK_DEV = 256
TRAJECTORY_TOKENS = 2048


def cluster_matches(key):
    cluster_locations = jax.random.randint(jax.random.fold_in(key, 4242), (2,), 0, TRAJECTORY_TOKENS)
    return jnp.any(jnp.arange(TRAJECTORY_TOKENS)[:, None] == cluster_locations[None, :], axis=1)


def draw_b_input(key, part):
    matched_entries = cluster_matches(key)
    baseline_values = 0.25 * jax.random.normal(jax.random.fold_in(key, 11), (TRAJECTORY_TOKENS, STATE), jnp.float32)
    baseline_values = jnp.clip(baseline_values, -1.5, 1.5)
    cluster_length = 0.00917 * TRAJECTORY_TOKENS
    return jnp.where(matched_entries[:, None], baseline_values / cluster_length, baseline_values).astype(jnp.bfloat16)


def draw_step_input(key, part):
    matched_entries = cluster_matches(key)
    uniform_part = jax.random.uniform(jax.random.fold_in(key, 21), (HEADS, TRAJECTORY_TOKENS), jnp.float32)
    baseline_values = -5.5 + 0.3 * uniform_part
    cluster_length = 0.00917 * TRAJECTORY_TOKENS
    return jnp.where(matched_entries[None, :], cluster_length, baseline_values)


def draw_decay_log(key, part):
    mean_step = 0.0131
    picker = jax.random.uniform(jax.random.fold_in(key, 31), (HEADS,), jnp.float32)
    slow_factor = jnp.exp(jax.random.uniform(jax.random.fold_in(key, 32), (HEADS,), jnp.float32, jnp.log(0.5), jnp.log(1.2)))
    middle_factor = jnp.exp(jax.random.uniform(jax.random.fold_in(key, 33), (HEADS,), jnp.float32, 0.0, jnp.log(3.0)))
    fast_factor = jnp.exp(jax.random.uniform(jax.random.fold_in(key, 34), (HEADS,), jnp.float32, jnp.log(0.02), jnp.log(0.08)))
    slow_rate = slow_factor * 0.6931 / (TRAJECTORY_TOKENS * mean_step)
    middle_rate = middle_factor / (TOK_DEV * mean_step)
    fast_rate = fast_factor / mean_step
    rate = jnp.where(picker < 0.5, slow_rate, jnp.where(picker < 0.75, middle_rate, fast_rate))
    return jnp.log(rate)


def draw_episode_end(key, part):
    silent_length = TRAJECTORY_TOKENS * 5 // 8
    silent_start = jax.random.randint(jax.random.fold_in(key, 51), (), 0, TRAJECTORY_TOKENS - silent_length + 1).astype(jnp.int32)
    position = jnp.arange(TRAJECTORY_TOKENS).astype(jnp.int32)
    sparse_ends = jax.random.randint(jax.random.fold_in(key, 52), (TRAJECTORY_TOKENS,), 0, TOK_DEV * 4) == 0
    silent_span = (position >= silent_start) & (position < silent_start + silent_length)
    planted = (position == silent_start - 1) | (position == silent_start + silent_length - 1)
    return jnp.where(sparse_ends & jnp.logical_not(silent_span) | planted, 1, 0).astype(jnp.int32)


def plant(values, own_key, low, largest):
    dims = values.shape
    index_at = [jax.random.randint(jax.random.fold_in(own_key, axis), (), 0, dims[axis]) for axis in range(len(dims))]
    values = values.at[tuple(index_at)].set(low)
    longest = dims.index(max(dims))
    index_at[longest] = (index_at[longest] + 1) % dims[longest]
    return values.at[tuple(index_at)].set(largest)


def levels(own_key, extent, cuts, low, top_value):
    loudness, own = 1.0, jax.random.fold_in(own_key, 6)
    for dim, blocks in cuts:
        steps = jnp.exp(jax.random.uniform(jax.random.fold_in(own, dim), (blocks,), jnp.float32, low / len(cuts), top_value / len(cuts)))
        loudness = loudness * jnp.repeat(steps, extent[dim] // blocks).reshape([-1 if axis == dim else 1 for axis in range(len(extent))])
    return loudness


def gaussian(own_key, dims, scale, limit, split=(), kind=jnp.bfloat16):
    values = jax.random.normal(own_key, dims, jnp.float32) * scale
    if len(split) > 0:
        values = levels(own_key, dims, split, -0.22, 0.18) * values
    return jnp.clip(values, min=-limit, max=limit).astype(kind)


def setup_inputs(seed: int = 0, part: int = 0) -> dict:
    arg_keys = jax.random.split(jax.random.key(seed), 12)
    part_splits = jax.random.split(jax.random.fold_in(arg_keys[11], part), 12)
    features = gaussian(part_splits[0], (TRAJECTORY_TOKENS, HEADS * HEAD_DIM), 1.0, 6.0, ((0, 8), (1, 2)))
    b_input = draw_b_input(jax.random.fold_in(jax.random.fold_in(arg_keys[11], part), 71), part)
    c_input = gaussian(part_splits[2], (TRAJECTORY_TOKENS, STATE), 0.25, 1.5, ((0, 8),))
    step_input = draw_step_input(jax.random.fold_in(jax.random.fold_in(arg_keys[11], part), 71), part)
    decay_log = draw_decay_log(jax.random.fold_in(arg_keys[11], 71), part)
    skip_gain = jnp.clip(0.5 + 1.5 * jax.random.uniform(arg_keys[5], (HEADS,), jnp.float32) ** levels(arg_keys[5], (HEADS,), ((0, 2),), -0.2, 0.2), 0.5, 2.0)
    norm_gain = jnp.clip(1.0 + 0.15 * jax.random.normal(arg_keys[6], (HEADS * HEAD_DIM,), jnp.float32), 0.25, 1.75)
    value_weight = gaussian(arg_keys[7], (HEADS * HEAD_DIM,), (HEADS * HEAD_DIM) ** -0.5, 0.125, ((0, 2),), jnp.float32)
    rewards = gaussian(part_splits[8], (TRAJECTORY_TOKENS,), 0.05, 0.3, ((0, 8),), jnp.float32)
    reward_keep_mask = plant((jax.random.randint(part_splits[9], (TRAJECTORY_TOKENS,), 0, 2) < 1).astype(jnp.int32), jax.random.fold_in(part_splits[9], 1), 0, 1)
    episode_end = draw_episode_end(jax.random.fold_in(jax.random.fold_in(arg_keys[11], part), 71), part)
    return {"features": features, "b_input": b_input, "c_input": c_input, "step_input": step_input, "decay_log": decay_log, "skip_gain": skip_gain, "norm_gain": norm_gain, "value_weight": value_weight, "rewards": rewards, "reward_keep_mask": reward_keep_mask, "episode_end": episode_end}


NORM_EPSILON = 1e-05
FULL_PRECISION = lax.Precision.HIGHEST

def reference(features, b_input, c_input, step_input, decay_log, skip_gain, norm_gain, value_weight, rewards, reward_keep_mask, episode_end):
    span_count = TRAJECTORY_TOKENS // SPAN
    row_width = HEADS * HEAD_DIM
    step_size = jax.nn.softplus(step_input)
    log_decay = (-jnp.exp(decay_log))[:, None] * step_size
    cumulative = jnp.cumsum(log_decay.reshape(HEADS, span_count, SPAN), axis=2)
    step_spans = step_size.reshape(HEADS, span_count, SPAN)
    readout = value_weight * norm_gain
    causal = jnp.arange(SPAN)[:, None] >= jnp.arange(SPAN)[None, :]

    def one_block(state, block):
        feat_block, key_block, query_block, cum_block, step_block = block
        feat_wide = feat_block.reshape(SPAN, HEADS, HEAD_DIM).astype(jnp.float32)
        scores = jnp.dot(query_block, key_block.T, preferred_element_type=jnp.float32)
        log_gap = jnp.where(causal[None], cum_block[:, :, None] - cum_block[:, None, :], 0.0)
        weights = jnp.where(causal[None], scores[None] * jnp.exp(log_gap) * step_block[:, None, :], 0.0)
        weights = lax.optimization_barrier(weights.astype(jnp.bfloat16)).astype(jnp.float32)
        intra = jnp.einsum('hts,shp->thp', weights, feat_wide, precision=FULL_PRECISION)
        carried = jnp.einsum('tn,hpn->thp', query_block.astype(jnp.float32), state, precision=FULL_PRECISION)
        carried = carried * jnp.exp(cum_block).T[:, :, None]
        block_total = cum_block[:, -1]
        coefficient = (jnp.exp(block_total[:, None] - cum_block) * step_block).T
        scaled = coefficient[:, :, None] * feat_wide
        scaled = lax.optimization_barrier(scaled.astype(jnp.bfloat16)).astype(jnp.float32)
        block_state = jnp.einsum('shp,sn->hpn', scaled, key_block.astype(jnp.float32), precision=FULL_PRECISION)
        new_state = jnp.exp(block_total)[:, None, None] * state + block_state
        mixed = (intra + carried + skip_gain[None, :, None] * feat_wide).reshape(SPAN, row_width)
        mean_square = lax.optimization_barrier(jnp.mean(mixed * mixed, axis=1))
        block_values = jnp.dot(mixed, readout, precision=FULL_PRECISION) / jnp.sqrt(mean_square + NORM_EPSILON)
        return (new_state, block_values)
    start_state = jnp.zeros((HEADS, HEAD_DIM, STATE), jnp.float32)
    blocks = (features.reshape(span_count, SPAN, row_width), b_input.reshape(span_count, SPAN, STATE), c_input.reshape(span_count, SPAN, STATE), jnp.transpose(cumulative, (1, 0, 2)), jnp.transpose(step_spans, (1, 0, 2)))
    final_state, value_blocks = lax.scan(one_block, start_state, blocks)
    values = value_blocks.reshape(TRAJECTORY_TOKENS)
    live_rewards = reward_keep_mask.astype(jnp.float32) * rewards
    keep_flags = 1.0 - episode_end.astype(jnp.float32)
    next_values = jnp.concatenate([values[1:], jnp.zeros((1,), jnp.float32)])
    delta = live_rewards + keep_flags * next_values - values

    def backward(carry_value, item):
        delta_here, keep_here = item
        result = delta_here + keep_here * carry_value
        return (result, result)
    final_carry, advantages = lax.scan(backward, jnp.zeros((), jnp.float32), (delta, keep_flags), reverse=True)
    return (values, advantages)
```

```python
import functools

import jax
import jax.numpy as jnp
from jax import lax
from jax.experimental import pallas as pl
from jax.experimental.pallas import tpu as pltpu
from jax.sharding import PartitionSpec as P

HEAD_DIM = 32
SPAN = 256
GROUP = 4
EXTRA = 8
NORM_EPSILON = 1e-05
VMEM_BYTES = 24 * 1024 * 1024


def split3(value):
    high = value.astype(jnp.bfloat16).astype(jnp.float32)
    rest = value - high
    middle = rest.astype(jnp.bfloat16).astype(jnp.float32)
    return high, middle, (rest - middle).astype(jnp.bfloat16).astype(jnp.float32)


def dot(a, b, contract=((1,), (0,))):
    return lax.dot_general(a, b, (contract, ((), ())), preferred_element_type=jnp.float32)


def iota(shape, dim):
    return lax.broadcasted_iota(jnp.int32, shape, dim)


def column(row):
    n = row.shape[1]
    return jnp.sum(jnp.where(iota((n, n), 0) == iota((n, n), 1), row, 0.0), axis=1, keepdims=True)


def over_channels(per_head, first_head, channels):
    heads = per_head.shape[0]
    match = iota((heads, channels), 0) == first_head + iota((heads, channels), 1) // HEAD_DIM
    return jnp.sum(jnp.where(match, per_head, 0.0), axis=0, keepdims=True)


def selector(heads, rows, first_head, channels):
    row = iota((rows, channels), 0)
    match = (lax.rem(row, heads) == first_head + iota((rows, channels), 1) // HEAD_DIM) & (row < 3 * heads)
    return jnp.where(match, 1.0, 0.0).astype(jnp.bfloat16)


def member_index():
    return lax.rem(lax.axis_index("ctx"), GROUP)


def state_kernel(step_in, decay_log, features, b_input, rewards, keep, ends, *outs):
    pieces, (cum_out, step_out, columns_out, row_out) = outs[:GROUP], outs[GROUP:]
    heads, span = step_in.shape
    state = b_input.shape[1]
    wide = features.shape[1] // GROUP
    raw = step_in[...]
    step = jnp.maximum(raw, 0.0) + jnp.log1p(jnp.exp(-jnp.abs(raw)))
    log_decay = -jnp.exp(column(decay_log[...])) * step
    ends_row = ends[...].astype(jnp.float32)
    live = keep[...].astype(jnp.float32) * rewards[...]
    upper = jnp.where(iota((span, span), 0) <= iota((span, span), 1), 1.0, 0.0).astype(jnp.bfloat16)
    stacked = jnp.concatenate(split3(log_decay) + (jnp.broadcast_to(ends_row, (16, span)),), axis=0)
    summed = dot(stacked.astype(jnp.bfloat16), upper)
    cum = summed[:heads] + summed[heads : 2 * heads] + summed[2 * heads : 3 * heads]
    through = summed[3 * heads : 3 * heads + 1]
    before = through - ends_row
    total = cum[:, span - 1 :]
    first_sum = jnp.sum(jnp.where(before == 0.0, live, 0.0), axis=1, keepdims=True)
    still_open = jnp.where(through[:, span - 1 :] == 0.0, 1.0, 0.0)
    coefficient = jnp.exp(total - cum) * step
    pad = jnp.zeros((128 - 3 * heads, span), jnp.float32)
    by_token = jnp.concatenate(split3(coefficient) + (pad,), axis=0).T.astype(jnp.bfloat16)
    cum_out[...] = cum
    step_out[...] = step
    columns_out[:, :128] = jnp.concatenate(split3(cum) + (jnp.ones_like(pad),), axis=0).T.astype(jnp.bfloat16)
    columns_out[:, 128:] = jnp.concatenate(split3(jnp.exp(cum)) + (pad,), axis=0).T.astype(jnp.bfloat16)
    row_out[...] = jnp.concatenate([live, ends_row, through, before, jnp.zeros((4, span), jnp.float32)], axis=0)
    keys = b_input[...]
    me = member_index()
    for j in range(GROUP):
        part = lax.bitwise_xor(me, j)
        first_head = part * (heads // GROUP)
        feat = features[:, pl.ds(pl.multiple_of(part * wide, wide), wide)]
        spread = dot(by_token, selector(heads, 128, first_head, wide))
        scaled = (spread * feat.astype(jnp.float32)).astype(jnp.bfloat16)
        pieces[j][:state, :] = dot(keys, scaled, ((0,), (0,)))
        row = iota((EXTRA, wide), 0)
        pieces[j][state:, :] = jnp.where(
            row == 0, over_channels(total, first_head, wide), jnp.where(row == 1, still_open, first_sum)
        )


def intra_kernel(features, b_input, c_input, cum_ref, step_ref, columns, rows, skip, out, suffix):
    heads, span = cum_ref.shape
    at_once = 128 // HEAD_DIM
    t, s = iota((span, span), 0), iota((span, span), 1)
    scores = jnp.where(t >= s, dot(c_input[...], b_input[...], ((1,), (1,))), 0.0)
    by_token = columns[:, :128]
    skip_row = over_channels(column(skip[...]), 0, heads * HEAD_DIM)
    out[...] = features[...].astype(jnp.float32) * skip_row
    row = iota((128, span), 0)

    def some_heads(index, carry):
        first = index * at_once
        lanes = pl.ds(pl.multiple_of(index * 128, 128), 128)
        feat = features[:, lanes]
        total = out[:, lanes]
        owner = iota((span, 128), 1) // HEAD_DIM
        for j in range(at_once):
            head = first + j
            cum = cum_ref[pl.ds(head, 1), :]
            high, middle, low = split3(cum)
            other = jnp.where(
                row < 3 * heads,
                jnp.where(lax.rem(row, heads) == head, 1.0, 0.0),
                jnp.where(
                    row == 3 * heads,
                    -high,
                    jnp.where(row == 3 * heads + 1, -middle, jnp.where(row == 3 * heads + 2, -low, 0.0)),
                ),
            ).astype(jnp.bfloat16)
            gap = jnp.minimum(dot(by_token, other), 0.0)
            weights = (scores * jnp.exp(gap) * step_ref[pl.ds(head, 1), :]).astype(jnp.bfloat16)
            total = total + dot(weights, jnp.where(owner == j, feat, jnp.zeros_like(feat)))
        out[:, lanes] = total
        return carry

    lax.fori_loop(0, heads // at_once, some_heads, 0)

    live, through, before = rows[0:1, :], rows[2:3, :], rows[3:4, :]
    reach = jnp.where((t >= s) & (column(before) == before), column(live), 0.0)
    sums = jnp.sum(reach, axis=0, keepdims=True)
    open_end = jnp.where(before == through[:, span - 1 :], 1.0, 0.0)
    suffix[...] = jnp.concatenate([sums, open_end, jnp.zeros((6, span), jnp.float32)], axis=0)


def in_order(pieces, me_static):
    return [pieces[me_static ^ m] for m in range(GROUP)]


def total_kernel(*refs):
    pieces, out = refs[:GROUP], refs[GROUP]
    state = pieces[0].shape[0] - EXTRA
    me = member_index()
    for v in range(GROUP):

        @pl.when(me == v)
        def _():
            members = in_order(pieces, v)
            running = members[0][:state, :]
            for piece in members[1:]:
                running = jnp.exp(piece[state : state + 1, :]) * running + piece[:state, :]
            out[:state, :] = running
            extra = [piece[state:, :] for piece in members]
            decay = functools.reduce(lambda a, b: a + b, [e[0:1] for e in extra])
            keeps = functools.reduce(lambda a, b: a * b, [e[1:2] for e in extra])
            amount = extra[-1][2:3]
            for e in extra[-2::-1]:
                amount = e[2:3] + e[1:2] * amount
            row = iota((EXTRA, decay.shape[1]), 0)
            out[state:, :] = jnp.where(row == 0, decay, jnp.where(row == 1, keeps, amount))


def round_kernel(bit, *refs):
    total, got, before, total_out, before_out = refs
    state = total.shape[0] - EXTRA
    group = lax.axis_index("ctx") // GROUP
    row = iota((EXTRA, total.shape[1]), 0)
    mine, theirs, past = total[state:, :], got[state:, :], before[state:, :]

    def rows(decay, keeps, amount):
        return jnp.where(row == 0, decay, jnp.where(row == 1, keeps, amount))

    decay, keeps = mine[0:1] + theirs[0:1], mine[1:2] * theirs[1:2]

    @pl.when(lax.rem(group // bit, 2) == 1)
    def _():
        before_out[:state, :] = before[:state, :] + jnp.exp(past[0:1]) * got[:state, :]
        before_out[state:, :] = rows(past[0:1] + theirs[0:1], past[1:2], past[2:3])
        total_out[:state, :] = total[:state, :] + jnp.exp(mine[0:1]) * got[:state, :]
        total_out[state:, :] = rows(decay, keeps, theirs[2:3] + theirs[1:2] * mine[2:3])

    @pl.when(lax.rem(group // bit, 2) == 0)
    def _():
        before_out[:state, :] = before[:state, :]
        before_out[state:, :] = rows(past[0:1], past[1:2] * theirs[1:2], past[2:3] + past[1:2] * theirs[2:3])
        total_out[:state, :] = got[:state, :] + jnp.exp(theirs[0:1]) * total[:state, :]
        total_out[state:, :] = rows(decay, keeps, mine[2:3] + mine[1:2] * theirs[2:3])


def entering_kernel(bit, has_past, *refs):
    pieces, got = refs[:GROUP], refs[GROUP]
    past = refs[GROUP + 1] if has_past else None
    outs, carry_out = refs[-GROUP - 1 : -1], refs[-1]
    state = got.shape[0] - EXTRA
    ctx = lax.axis_index("ctx")
    me = lax.rem(ctx, GROUP)
    is_later = lax.rem(ctx // GROUP // bit, 2) == 1
    theirs = got[state:, :]
    for v in range(GROUP):

        @pl.when(me == v)
        def _():
            members = in_order(pieces, v)
            arriving = jnp.where(is_later, got[:state, :], 0.0)
            amount = jnp.where(is_later, 0.0, theirs[2:3])
            if has_past:
                old = past[state:, :]
                arriving = past[:state, :] + jnp.exp(old[0:1]) * arriving
                amount = old[2:3] + old[1:2] * amount
            for m in range(GROUP):
                outs[v ^ m][...] = arriving
                if m < GROUP - 1:
                    piece = members[m]
                    arriving = jnp.exp(piece[state : state + 1, :]) * arriving + piece[:state, :]
            for m in range(GROUP - 1, v, -1):
                extra = members[m][state:, :]
                amount = extra[2:3] + extra[1:2] * amount
            carry_out[...] = jnp.broadcast_to(amount, carry_out.shape)


def readout_kernel(*refs):
    entering, (c_input, columns, inside, weight, gain, out) = refs[:GROUP], refs[GROUP:]
    state, wide = entering[0].shape
    span = c_input.shape[0]
    heads = inside.shape[1] // HEAD_DIM
    me = member_index()
    queries = c_input[...]
    by_token = columns[:, 128:]
    squares = jnp.zeros((span, 128), jnp.float32)
    values = jnp.zeros((span, 128), jnp.float32)
    for j in range(GROUP):
        part = lax.bitwise_xor(me, j)
        lanes = pl.ds(pl.multiple_of(part * wide, wide), wide)
        value = entering[j][...]
        high = value.astype(jnp.bfloat16)
        low = (value - high.astype(jnp.float32)).astype(jnp.bfloat16)
        carried = dot(queries, high) + dot(queries, low)
        decay = dot(by_token, selector(heads, 128, part * (heads // GROUP), wide))
        mixed = inside[:, lanes] + carried * decay
        readout = weight[:, lanes] * gain[:, lanes]
        squared, read = mixed * mixed, mixed * readout
        for k in range(0, wide, 128):
            squares = squares + squared[:, k : k + 128]
            values = values + read[:, k : k + 128]
    out[0:1, :] = jnp.sum(squares.T, axis=0, keepdims=True)
    out[1:2, :] = jnp.sum(values.T, axis=0, keepdims=True)


def call(kernel, shapes, name, *args):
    single = not isinstance(shapes, (list, tuple))
    structs = [jax.ShapeDtypeStruct(s, d) for s, d in ([shapes] if single else shapes)]
    result = pl.pallas_call(
        kernel,
        out_shape=structs,
        in_specs=[pl.BlockSpec(memory_space=pltpu.VMEM)] * len(args),
        out_specs=[pl.BlockSpec(memory_space=pltpu.VMEM)] * len(structs),
        compiler_params=pltpu.CompilerParams(vmem_limit_bytes=VMEM_BYTES),
        name=name,
    )(*args)
    return result


def swap(value, axis, mask):
    count = lax.axis_size(axis)
    return lax.ppermute(value, axis, [(k, k ^ mask) for k in range(count)])


def local(
    features,
    b_input,
    c_input,
    step_input,
    decay_log,
    skip_gain,
    norm_gain,
    value_weight,
    rewards,
    reward_keep_mask,
    episode_end,
):
    span, width = features.shape
    heads = step_input.shape[0]
    state = b_input.shape[1]
    wide = width // GROUP
    count = lax.axis_size("ctx")
    groups = count // GROUP
    assert span == SPAN and count == groups * GROUP and groups > 1 and groups & (groups - 1) == 0
    f32, bf16 = jnp.float32, jnp.bfloat16
    piece = ((state + EXTRA, wide), f32)

    made = call(
        state_kernel,
        [piece] * GROUP
        + [((heads, span), f32), ((heads, span), f32), ((span, 256), bf16), ((8, span), f32)],
        "block_states",
        step_input,
        decay_log[None, :],
        features,
        b_input,
        rewards[None, :],
        reward_keep_mask[None, :],
        episode_end[None, :],
    )
    pieces, (cum, step, columns, rows) = made[:GROUP], made[GROUP:]
    got = [pieces[0]] + [swap(pieces[j], "ctx", j) for j in range(1, GROUP)]
    inside, suffix = call(
        intra_kernel,
        [((span, width), f32), ((8, span), f32)],
        "inside_block",
        features,
        b_input,
        c_input,
        cum,
        step,
        columns,
        rows,
        skip_gain[None, :],
    )
    (total,) = call(total_kernel, [piece], "group_total", *got)
    past = None
    bit = 1
    while bit * 2 < groups:
        other = swap(total, "ctx", GROUP * bit)
        if past is None:
            row = jnp.arange(state + EXTRA)[:, None]
            past = jnp.where(row == state + 1, 1.0, 0.0).astype(f32) * jnp.ones((1, wide), f32)
        total, past = call(
            functools.partial(round_kernel, bit), [piece, piece], "scan_round", total, other, past
        )
        bit *= 2
    other = swap(total, "ctx", GROUP * bit)
    made = call(
        functools.partial(entering_kernel, bit, past is not None),
        [((state, wide), f32)] * GROUP + [((8, wide), f32)],
        "entering_states",
        *got,
        other,
        *([] if past is None else [past]),
    )
    entering, carry = made[:GROUP], made[GROUP]
    arrived = [entering[0]] + [swap(entering[j], "ctx", j) for j in range(1, GROUP)]
    (sums,) = call(
        readout_kernel,
        [((2, span), f32)],
        "readout",
        *arrived,
        c_input,
        columns,
        inside,
        value_weight[None, :],
        norm_gain[None, :],
    )
    sums = sums + swap(sums, "head", 1)
    mean_square = sums[0] / (width * lax.axis_size("head"))
    values = sums[1] / jnp.sqrt(mean_square + NORM_EPSILON)
    returns = suffix[0] + suffix[1] * carry[0, 0]
    return (values, returns - values)


def solution(mesh):
    placed = (
        P(("traj", "ctx"), "head"),
        P(("traj", "ctx"), None),
        P(("traj", "ctx"), None),
        P("head", ("traj", "ctx")),
        P("head"),
        P("head"),
        P("head"),
        P("head"),
        P(("traj", "ctx")),
        P(("traj", "ctx")),
        P(("traj", "ctx")),
    )
    return jax.shard_map(
        local,
        mesh=mesh,
        in_specs=placed,
        out_specs=(P(("traj", "ctx")), P(("traj", "ctx"))),
        check_vma=False,
    )
```

```python
import functools

import jax
import jax.numpy as jnp
from jax import lax
from jax.experimental import pallas as pl
from jax.experimental.pallas import tpu as pltpu
from jax.sharding import PartitionSpec as P

HEAD_DIM = 32
SPAN = 256
GROUP = 4
EXTRA = 8
NORM_EPSILON = 1e-05
VMEM_BYTES = 24 * 1024 * 1024


def split3(value):
    high = value.astype(jnp.bfloat16).astype(jnp.float32)
    rest = value - high
    middle = rest.astype(jnp.bfloat16).astype(jnp.float32)
    return high, middle, (rest - middle).astype(jnp.bfloat16).astype(jnp.float32)


def dot(a, b, contract=((1,), (0,))):
    return lax.dot_general(a, b, (contract, ((), ())), preferred_element_type=jnp.float32)


def iota(shape, dim):
    return lax.broadcasted_iota(jnp.int32, shape, dim)


def column(row):
    n = row.shape[1]
    return jnp.sum(jnp.where(iota((n, n), 0) == iota((n, n), 1), row, 0.0), axis=1, keepdims=True)


def over_channels(per_head, first_head, channels):
    heads = per_head.shape[0]
    match = iota((heads, channels), 0) == first_head + iota((heads, channels), 1) // HEAD_DIM
    return jnp.sum(jnp.where(match, per_head, 0.0), axis=0, keepdims=True)


def selector(heads, rows, first_head, channels):
    row = iota((rows, channels), 0)
    match = (lax.rem(row, heads) == first_head + iota((rows, channels), 1) // HEAD_DIM) & (row < 3 * heads)
    return jnp.where(match, 1.0, 0.0).astype(jnp.bfloat16)


def member_index():
    return lax.rem(lax.axis_index("ctx"), GROUP)


def state_kernel(*refs):
    sources, refs = refs[:11], refs[11:]
    pieces, refs = refs[:GROUP], refs[GROUP:]
    features, b_input, c_input, cum_out, step_out, columns_out, row_out, wide_out = refs[:8]
    step_in, decay_log, skip_gain, norm_gain, value_weight, rewards, keep, ends, sems = refs[8:]
    targets = (step_in, decay_log, rewards, keep, ends, features, b_input, c_input, skip_gain, norm_gain, value_weight)
    copies = [pltpu.make_async_copy(src, dst, sems.at[i]) for i, (src, dst) in enumerate(zip(sources, targets))]
    for copy in copies:
        copy.start()
    heads, span = step_in.shape
    state = b_input.shape[1]
    wide = features.shape[1] // GROUP
    for copy in copies[:5]:
        copy.wait()
    raw = step_in[...]
    step = jnp.maximum(raw, 0.0) + jnp.log1p(jnp.exp(-jnp.abs(raw)))
    log_decay = -jnp.exp(column(decay_log[...])) * step
    ends_row = ends[...].astype(jnp.float32)
    live = keep[...].astype(jnp.float32) * rewards[...]
    upper = jnp.where(iota((span, span), 0) <= iota((span, span), 1), 1.0, 0.0).astype(jnp.bfloat16)
    stacked = jnp.concatenate(split3(log_decay) + (jnp.broadcast_to(ends_row, (16, span)),), axis=0)
    summed = dot(stacked.astype(jnp.bfloat16), upper)
    cum = summed[:heads] + summed[heads : 2 * heads] + summed[2 * heads : 3 * heads]
    through = summed[3 * heads : 3 * heads + 1]
    before = through - ends_row
    total = cum[:, span - 1 :]
    first_sum = jnp.sum(jnp.where(before == 0.0, live, 0.0), axis=1, keepdims=True)
    still_open = jnp.where(through[:, span - 1 :] == 0.0, 1.0, 0.0)
    coefficient = jnp.exp(total - cum) * step
    pad = jnp.zeros((128 - 3 * heads, span), jnp.float32)
    by_token = jnp.concatenate(split3(coefficient) + (pad,), axis=0).T.astype(jnp.bfloat16)
    for copy in copies[5:]:
        copy.wait()
    keys = b_input[...]
    me = member_index()
    for j in (1, 2, 3, 0):
        part = lax.bitwise_xor(me, j)
        first_head = part * (heads // GROUP)
        feat = features[:, pl.ds(pl.multiple_of(part * wide, wide), wide)]
        spread = dot(by_token, selector(heads, 128, first_head, wide))
        scaled = (spread * feat.astype(jnp.float32)).astype(jnp.bfloat16)
        pieces[j][:state, :] = dot(keys, scaled, ((0,), (0,)))
        row = iota((EXTRA, wide), 0)
        pieces[j][state:, :] = jnp.where(
            row == 0, over_channels(total, first_head, wide), jnp.where(row == 1, still_open, first_sum)
        )
    cum_out[...] = cum
    step_out[...] = step
    row_out[...] = jnp.concatenate([live, ends_row, through, before, jnp.zeros((4, span), jnp.float32)], axis=0)
    columns_out[:, :128] = jnp.concatenate(split3(cum) + (jnp.ones_like(pad),), axis=0).T.astype(jnp.bfloat16)
    columns_out[:, 128:] = jnp.concatenate(split3(jnp.exp(cum)) + (pad,), axis=0).T.astype(jnp.bfloat16)
    wide_out[0:1, :] = norm_gain[...] * value_weight[...]
    wide_out[1:2, :] = over_channels(column(skip_gain[...]), 0, heads * HEAD_DIM)


def intra_kernel(start, stop, features, b_input, c_input, cum_ref, step_ref, columns, rows, wide_row, *outs):
    out = outs[0]
    heads, span = cum_ref.shape
    at_once = 128 // HEAD_DIM
    t, s = iota((span, span), 0), iota((span, span), 1)
    scores = jnp.where(t >= s, dot(c_input[...], b_input[...], ((1,), (1,))), 0.0)
    by_token = columns[:, :128]
    row = iota((128, span), 0)

    def some_heads(index, carry):
        first = index * at_once
        lanes = pl.ds(pl.multiple_of(index * 128, 128), 128)
        here = pl.ds(pl.multiple_of((index - start) * 128, 128), 128)
        feat = features[:, lanes]
        total = feat.astype(jnp.float32) * wide_row[1:2, lanes]
        owner = iota((span, 128), 1) // HEAD_DIM
        for j in range(at_once):
            head = first + j
            cum = cum_ref[pl.ds(head, 1), :]
            high, middle, low = split3(cum)
            other = jnp.where(
                row < 3 * heads,
                jnp.where(lax.rem(row, heads) == head, 1.0, 0.0),
                jnp.where(
                    row == 3 * heads,
                    -high,
                    jnp.where(row == 3 * heads + 1, -middle, jnp.where(row == 3 * heads + 2, -low, 0.0)),
                ),
            ).astype(jnp.bfloat16)
            gap = jnp.minimum(dot(by_token, other), 0.0)
            weights = (scores * jnp.exp(gap) * step_ref[pl.ds(head, 1), :]).astype(jnp.bfloat16)
            total = total + dot(weights, jnp.where(owner == j, feat, jnp.zeros_like(feat)))
        out[:, here] = total
        return carry

    lax.fori_loop(start, stop, some_heads, 0)

    if len(outs) > 1:
        live, through, before = rows[0:1, :], rows[2:3, :], rows[3:4, :]
        reach = jnp.where((t >= s) & (column(before) == before), column(live), 0.0)
        sums = jnp.sum(reach, axis=0, keepdims=True)
        open_end = jnp.where(before == through[:, span - 1 :], 1.0, 0.0)
        outs[1][...] = jnp.concatenate([sums, open_end, jnp.zeros((6, span), jnp.float32)], axis=0)


def in_order(pieces, me_static):
    return [pieces[me_static ^ m] for m in range(GROUP)]


def total_kernel(*refs):
    pieces, out = refs[:GROUP], refs[-1]
    state = pieces[0].shape[0] - EXTRA
    me = member_index()
    for v in range(GROUP):

        @pl.when(me == v)
        def _():
            members = in_order(pieces, v)
            running = members[0][:state, :]
            for piece in members[1:]:
                running = jnp.exp(piece[state : state + 1, :]) * running + piece[:state, :]
            out[:state, :] = running
            extra = [piece[state:, :] for piece in members]
            decay = functools.reduce(lambda a, b: a + b, [e[0:1] for e in extra])
            keeps = functools.reduce(lambda a, b: a * b, [e[1:2] for e in extra])
            amount = extra[-1][2:3]
            for e in extra[-2::-1]:
                amount = e[2:3] + e[1:2] * amount
            row = iota((EXTRA, decay.shape[1]), 0)
            out[state:, :] = jnp.where(row == 0, decay, jnp.where(row == 1, keeps, amount))


def round_kernel(bit, *refs):
    total, got, before, total_out, before_out = refs
    state = total.shape[0] - EXTRA
    group = lax.axis_index("ctx") // GROUP
    row = iota((EXTRA, total.shape[1]), 0)
    mine, theirs, past = total[state:, :], got[state:, :], before[state:, :]

    def rows(decay, keeps, amount):
        return jnp.where(row == 0, decay, jnp.where(row == 1, keeps, amount))

    decay, keeps = mine[0:1] + theirs[0:1], mine[1:2] * theirs[1:2]

    @pl.when(lax.rem(group // bit, 2) == 1)
    def _():
        before_out[:state, :] = before[:state, :] + jnp.exp(past[0:1]) * got[:state, :]
        before_out[state:, :] = rows(past[0:1] + theirs[0:1], past[1:2], past[2:3])
        total_out[:state, :] = total[:state, :] + jnp.exp(mine[0:1]) * got[:state, :]
        total_out[state:, :] = rows(decay, keeps, theirs[2:3] + theirs[1:2] * mine[2:3])

    @pl.when(lax.rem(group // bit, 2) == 0)
    def _():
        before_out[:state, :] = before[:state, :]
        before_out[state:, :] = rows(past[0:1], past[1:2] * theirs[1:2], past[2:3] + past[1:2] * theirs[2:3])
        total_out[:state, :] = got[:state, :] + jnp.exp(theirs[0:1]) * total[:state, :]
        total_out[state:, :] = rows(decay, keeps, mine[2:3] + mine[1:2] * theirs[2:3])


def entering_kernel(bit, has_past, *refs):
    pieces, got = refs[:GROUP], refs[GROUP]
    past = refs[GROUP + 1] if has_past else None
    outs, carry_out = refs[-GROUP - 1 : -1], refs[-1]
    state = got.shape[0] - EXTRA
    ctx = lax.axis_index("ctx")
    me = lax.rem(ctx, GROUP)
    is_later = lax.rem(ctx // GROUP // bit, 2) == 1
    theirs = got[state:, :]
    for v in range(GROUP):

        @pl.when(me == v)
        def _():
            members = in_order(pieces, v)
            arriving = jnp.where(is_later, got[:state, :], 0.0)
            amount = jnp.where(is_later, 0.0, theirs[2:3])
            if has_past:
                old = past[state:, :]
                arriving = past[:state, :] + jnp.exp(old[0:1]) * arriving
                amount = old[2:3] + old[1:2] * amount
            for m in range(GROUP):
                outs[v ^ m][...] = arriving
                if m < GROUP - 1:
                    piece = members[m]
                    arriving = jnp.exp(piece[state : state + 1, :]) * arriving + piece[:state, :]
            for m in range(GROUP - 1, v, -1):
                extra = members[m][state:, :]
                amount = extra[2:3] + extra[1:2] * amount
            carry_out[...] = jnp.broadcast_to(amount, carry_out.shape)


def readout_kernel(*refs):
    entering, (c_input, columns, first_half, second_half, wide_row, out) = refs[:GROUP], refs[GROUP:]
    state, wide = entering[0].shape
    span = c_input.shape[0]
    heads = wide_row.shape[1] // HEAD_DIM
    me = member_index()
    queries = c_input[...]
    by_token = columns[:, 128:]
    squares = jnp.zeros((span, 128), jnp.float32)
    values = jnp.zeros((span, 128), jnp.float32)
    for j in range(GROUP):
        part = lax.bitwise_xor(me, j)
        half = pl.ds(pl.multiple_of(lax.rem(part, GROUP // 2) * wide, wide), wide)
        value = entering[j][...]
        high = value.astype(jnp.bfloat16)
        low = (value - high.astype(jnp.float32)).astype(jnp.bfloat16)
        carried = dot(queries, high) + dot(queries, low)
        decay = dot(by_token, selector(heads, 128, part * (heads // GROUP), wide))
        inside = jnp.where(part < GROUP // 2, first_half[:, half], second_half[:, half])
        mixed = inside + carried * decay
        readout = wide_row[0:1, pl.ds(pl.multiple_of(part * wide, wide), wide)]
        squared, read = mixed * mixed, mixed * readout
        for k in range(0, wide, 128):
            squares = squares + squared[:, k : k + 128]
            values = values + read[:, k : k + 128]
    out[0:1, :] = jnp.sum(squares.T, axis=0, keepdims=True)
    out[1:2, :] = jnp.sum(values.T, axis=0, keepdims=True)


def last_kernel(channels, mine, other, suffix, carry, values_out, advantages_out, values, advantages, sems):
    sums = mine[...] + other[...]
    value = sums[1:2] / jnp.sqrt(sums[0:1] / channels + NORM_EPSILON)
    values[...] = value
    advantages[...] = suffix[0:1, :] + suffix[1:2, :] * carry[0:1, 0:1] - value
    copies = [
        pltpu.make_async_copy(values, values_out, sems.at[0]),
        pltpu.make_async_copy(advantages, advantages_out, sems.at[1]),
    ]
    for copy in copies:
        copy.start()
    for copy in copies:
        copy.wait()


def call(kernel, shapes, name, *args, hbm_in=False, hbm_out=False, scratch=()):
    near, far = pl.BlockSpec(memory_space=pltpu.VMEM), pl.BlockSpec(memory_space=pltpu.HBM)
    if hbm_in:
        args = [pltpu.with_memory_space_constraint(arg, pltpu.HBM) for arg in args]
    return pl.pallas_call(
        kernel,
        out_shape=[jax.ShapeDtypeStruct(*shape) for shape in shapes],
        in_specs=[far if hbm_in else near] * len(args),
        out_specs=[far if hbm_out else near] * len(shapes),
        scratch_shapes=scratch,
        compiler_params=pltpu.CompilerParams(vmem_limit_bytes=VMEM_BYTES),
        name=name,
    )(*args)


def swap(value, axis, mask):
    count = lax.axis_size(axis)
    return lax.ppermute(value, axis, [(k, k ^ mask) for k in range(count)])


def local(
    features,
    b_input,
    c_input,
    step_input,
    decay_log,
    skip_gain,
    norm_gain,
    value_weight,
    rewards,
    reward_keep_mask,
    episode_end,
):
    span, width = features.shape
    heads = step_input.shape[0]
    state = b_input.shape[1]
    wide = width // GROUP
    count = lax.axis_size("ctx")
    groups = count // GROUP
    assert span == SPAN and count == groups * GROUP and groups > 1 and groups & (groups - 1) == 0
    f32, bf16 = jnp.float32, jnp.bfloat16
    piece = ((state + EXTRA, wide), f32)

    i32 = jnp.int32
    made = call(
        state_kernel,
        [piece] * GROUP
        + [
            ((span, width), bf16),
            ((span, state), bf16),
            ((span, state), bf16),
            ((heads, span), f32),
            ((heads, span), f32),
            ((span, 256), bf16),
            ((8, span), f32),
            ((2, width), f32),
        ],
        "block_states",
        step_input,
        decay_log[None, :],
        rewards[None, :],
        reward_keep_mask[None, :],
        episode_end[None, :],
        features,
        b_input,
        c_input,
        skip_gain[None, :],
        norm_gain[None, :],
        value_weight[None, :],
        hbm_in=True,
        scratch=[
            pltpu.VMEM((heads, span), f32),
            pltpu.VMEM((1, heads), f32),
            pltpu.VMEM((1, heads), f32),
            pltpu.VMEM((1, width), f32),
            pltpu.VMEM((1, width), f32),
            pltpu.VMEM((1, span), f32),
            pltpu.VMEM((1, span), i32),
            pltpu.VMEM((1, span), i32),
            pltpu.SemaphoreType.DMA((11,)),
        ],
    )
    pieces, near = made[:GROUP], made[GROUP:]
    queries, columns, wide_row = near[2], near[5], near[7]
    got = [pieces[0]] + [swap(pieces[j], "ctx", j) for j in range(1, GROUP)]
    head_groups = heads * HEAD_DIM // 128
    half = head_groups // 2
    half_shape = ((span, width // 2), f32)
    first_half, suffix = call(
        functools.partial(intra_kernel, 0, half), [half_shape, ((8, span), f32)], "inside_first", *near
    )
    (total,) = call(total_kernel, [piece], "group_total", *got, suffix)
    past = None
    bit = 1
    while bit * 2 < groups:
        other = swap(total, "ctx", GROUP * bit)
        if past is None:
            row = jnp.arange(state + EXTRA)[:, None]
            past = jnp.where(row == state + 1, 1.0, 0.0).astype(f32) * jnp.ones((1, wide), f32)
        total, past = call(
            functools.partial(round_kernel, bit), [piece, piece], "scan_round", total, other, past
        )
        bit *= 2
    other = swap(total, "ctx", GROUP * bit)
    (second_half,) = call(
        functools.partial(intra_kernel, half, head_groups), [half_shape], "inside_second", *near
    )
    made = call(
        functools.partial(entering_kernel, bit, past is not None),
        [((state, wide), f32)] * GROUP + [((8, wide), f32)],
        "entering_states",
        *got,
        other,
        *([] if past is None else [past]),
        second_half,
    )
    entering, carry = made[:GROUP], made[GROUP]
    arrived = [entering[0]] + [swap(entering[j], "ctx", j) for j in range(1, GROUP)]
    (sums,) = call(
        readout_kernel, [((2, span), f32)], "readout", *arrived, queries, columns, first_half, second_half, wide_row
    )
    values, advantages = call(
        functools.partial(last_kernel, width * lax.axis_size("head")),
        [((1, span), f32)] * 2,
        "values_and_advantages",
        sums,
        swap(sums, "head", 1),
        suffix,
        carry,
        hbm_out=True,
        scratch=[pltpu.VMEM((1, span), f32), pltpu.VMEM((1, span), f32), pltpu.SemaphoreType.DMA((2,))],
    )
    return (values[0], advantages[0])


def solution(mesh):
    placed = (
        P(("traj", "ctx"), "head"),
        P(("traj", "ctx"), None),
        P(("traj", "ctx"), None),
        P("head", ("traj", "ctx")),
        P("head"),
        P("head"),
        P("head"),
        P("head"),
        P(("traj", "ctx")),
        P(("traj", "ctx")),
        P(("traj", "ctx")),
    )
    return jax.shard_map(
        local,
        mesh=mesh,
        in_specs=placed,
        out_specs=(P(("traj", "ctx")), P(("traj", "ctx"))),
        check_vma=False,
    )
```

```python
import functools

import jax
import jax.numpy as jnp
from jax import lax
from jax.experimental import pallas as pl
from jax.experimental.pallas import tpu as pltpu
from jax.sharding import PartitionSpec as P

HEAD_DIM = 32
SPAN = 256
GROUP = 4
LANES = 128
LATE = 0
SHARES = ((0, 2, 2, 8, 8), (0, 0, 4, 8, 8))
EXTRA = 8
NORM_EPSILON = 1e-05
VMEM_BYTES = 24 * 1024 * 1024


def split3(value):
    high = value.astype(jnp.bfloat16).astype(jnp.float32)
    rest = value - high
    middle = rest.astype(jnp.bfloat16).astype(jnp.float32)
    return high, middle, (rest - middle).astype(jnp.bfloat16).astype(jnp.float32)


def dot(a, b, contract=((1,), (0,))):
    return lax.dot_general(a, b, (contract, ((), ())), preferred_element_type=jnp.float32)


def iota(shape, dim):
    return lax.broadcasted_iota(jnp.int32, shape, dim)


def column(row):
    n = row.shape[1]
    return jnp.sum(jnp.where(iota((n, n), 0) == iota((n, n), 1), row, 0.0), axis=1, keepdims=True)


def over_channels(per_head, first_head, channels):
    heads = per_head.shape[0]
    match = iota((heads, channels), 0) == first_head + iota((heads, channels), 1) // HEAD_DIM
    return jnp.sum(jnp.where(match, per_head, 0.0), axis=0, keepdims=True)


def selector(heads, rows, first_head, channels):
    row = iota((rows, channels), 0)
    match = (lax.rem(row, heads) == first_head + iota((rows, channels), 1) // HEAD_DIM) & (row < 3 * heads)
    return jnp.where(match, 1.0, 0.0).astype(jnp.bfloat16)


def is_late():
    return lax.axis_index("head") == LATE


def member_index():
    return lax.rem(lax.axis_index("ctx"), GROUP)


def prepare(cum_ref, skip, norm, weight, columns_out, wide_out):
    heads, span = cum_ref.shape
    cum = cum_ref[...]
    pad = jnp.zeros((128 - 3 * heads, span), jnp.float32)
    columns_out[:, :128] = jnp.concatenate(split3(cum) + (jnp.ones_like(pad),), axis=0).T.astype(jnp.bfloat16)
    columns_out[:, 128:] = jnp.concatenate(split3(jnp.exp(cum)) + (pad,), axis=0).T.astype(jnp.bfloat16)
    wide_out[0:1, :] = norm[...] * weight[...]
    wide_out[1:2, :] = over_channels(column(skip[...]), 0, heads * HEAD_DIM)


def state_kernel(*refs):
    sources, refs = refs[:11], refs[11:]
    pieces, refs = refs[:GROUP], refs[GROUP:]
    features, b_input, c_input, cum_out, step_out, rows, skip, norm, weight, columns, wide_row, inside = refs[:12]
    step_in, decay_log, rewards, keep, ends, sems = refs[12:]
    targets = (step_in, decay_log, rewards, keep, ends, features, b_input, c_input, skip, norm, weight)
    copies = [pltpu.make_async_copy(src, dst, sems.at[i]) for i, (src, dst) in enumerate(zip(sources, targets))]
    for copy in copies:
        copy.start()
    heads, span = step_in.shape
    state = b_input.shape[1]
    wide = features.shape[1] // GROUP
    for copy in copies[:5]:
        copy.wait()
    raw = step_in[...]
    step = jnp.maximum(raw, 0.0) + jnp.log1p(jnp.exp(-jnp.abs(raw)))
    log_decay = -jnp.exp(column(decay_log[...])) * step
    ends_row = ends[...].astype(jnp.float32)
    live = keep[...].astype(jnp.float32) * rewards[...]
    upper = jnp.where(iota((span, span), 0) <= iota((span, span), 1), 1.0, 0.0).astype(jnp.bfloat16)
    stacked = jnp.concatenate(split3(log_decay) + (jnp.broadcast_to(ends_row, (16, span)),), axis=0)
    summed = dot(stacked.astype(jnp.bfloat16), upper)
    cum = summed[:heads] + summed[heads : 2 * heads] + summed[2 * heads : 3 * heads]
    through = summed[3 * heads : 3 * heads + 1]
    before = through - ends_row
    total = cum[:, span - 1 :]
    first_sum = jnp.sum(jnp.where(before == 0.0, live, 0.0), axis=1, keepdims=True)
    still_open = jnp.where(through[:, span - 1 :] == 0.0, 1.0, 0.0)
    coefficient = jnp.exp(total - cum) * step
    pad = jnp.zeros((128 - 3 * heads, span), jnp.float32)
    by_token = jnp.concatenate(split3(coefficient) + (pad,), axis=0).T.astype(jnp.bfloat16)
    cum_out[...] = cum
    step_out[...] = step
    rows[...] = jnp.concatenate([live, through, before, jnp.zeros((5, span), jnp.float32)], axis=0)
    for copy in copies[5:]:
        copy.wait()

    @pl.when(is_late())
    def _():
        prepare(cum_out, skip, norm, weight, columns, wide_row)
        intra_groups(0, features, b_input, c_input, cum_out, step_out, columns, wide_row, inside)

    keys = b_input[...].T
    me = member_index()
    row = iota((EXTRA, LANES), 0)
    for j in (1, 2, 3, 0):
        part = lax.bitwise_xor(me, j)
        first_head = part * (heads // GROUP)
        feat = features[:, pl.ds(pl.multiple_of(part * wide, wide), wide)]
        spread = dot(by_token, selector(heads, 128, first_head, wide))
        scaled = (spread * feat.astype(jnp.float32)).astype(jnp.bfloat16)
        states = dot(keys, scaled)
        decay = over_channels(total, first_head, wide)
        extra = jnp.where(row == wide // LANES, still_open, first_sum)
        for k in range(wide // LANES):
            pieces[j][k * state : (k + 1) * state, :] = states[:, k * LANES : (k + 1) * LANES]
            extra = jnp.where(row == k, decay[:, k * LANES : (k + 1) * LANES], extra)
        pieces[j][wide // LANES * state :, :] = extra


def intra_groups(stage, features, b_input, c_input, cum_ref, step_ref, columns, wide_row, out):
    start, stop = (jnp.where(is_late(), SHARES[0][k], SHARES[1][k]) for k in (stage, stage + 1))
    heads, span = cum_ref.shape
    at_once = 128 // HEAD_DIM
    t, s = iota((span, span), 0), iota((span, span), 1)
    scores = jnp.where(t >= s, dot(c_input[...], b_input[...], ((1,), (1,))), 0.0)
    by_token = columns[:, :128]
    row = iota((128, span), 0)

    def some_heads(index, carry):
        first = index * at_once
        lanes = pl.ds(pl.multiple_of(index * 128, 128), 128)
        feat = features[:, lanes]
        total = feat.astype(jnp.float32) * wide_row[1:2, lanes]
        owner = iota((span, 128), 1) // HEAD_DIM
        for j in range(at_once):
            head = first + j
            cum = cum_ref[pl.ds(head, 1), :]
            high, middle, low = split3(cum)
            other = jnp.where(
                row < 3 * heads,
                jnp.where(lax.rem(row, heads) == head, 1.0, 0.0),
                jnp.where(
                    row == 3 * heads,
                    -high,
                    jnp.where(row == 3 * heads + 1, -middle, jnp.where(row == 3 * heads + 2, -low, 0.0)),
                ),
            ).astype(jnp.bfloat16)
            gap = jnp.minimum(dot(by_token, other), 0.0)
            weights = (scores * jnp.exp(gap) * step_ref[pl.ds(head, 1), :]).astype(jnp.bfloat16)
            total = total + dot(weights, jnp.where(owner == j, feat, jnp.zeros_like(feat)))
        out[:, lanes] = total
        return carry

    lax.fori_loop(start, stop, some_heads, 0)


def first_kernel(
    features, b_input, c_input, cum_ref, step_ref, rows, skip, norm, weight, _0, _1, _2, columns, wide_row, out, suffix
):
    @pl.when(jnp.logical_not(is_late()))
    def _():
        prepare(cum_ref, skip, norm, weight, columns, wide_row)

    intra_groups(1, features, b_input, c_input, cum_ref, step_ref, columns, wide_row, out)

    span = cum_ref.shape[1]
    t, s = iota((span, span), 0), iota((span, span), 1)
    live, through, before = rows[0:1, :], rows[1:2, :], rows[2:3, :]
    reach = jnp.where((t >= s) & (column(before) == before), column(live), 0.0)
    sums = jnp.sum(reach, axis=0, keepdims=True)
    open_end = jnp.where(before == through[:, span - 1 :], 1.0, 0.0)
    suffix[...] = jnp.concatenate([sums, open_end, jnp.zeros((6, span), jnp.float32)], axis=0)


def second_kernel(features, b_input, c_input, cum_ref, step_ref, columns, wide_row, _, out):
    intra_groups(2, features, b_input, c_input, cum_ref, step_ref, columns, wide_row, out)


def in_order(pieces, me_static):
    return [pieces[me_static ^ m] for m in range(GROUP)]


def parts_of(piece):
    halves = 2
    size = (piece.shape[0] - EXTRA) // halves
    extra = piece[halves * size :, :]
    return (
        [piece[k * size : (k + 1) * size, :] for k in range(halves)],
        [extra[k : k + 1] for k in range(halves)],
        extra[halves : halves + 1],
        extra[halves + 1 : halves + 2],
    )


def write_piece(out, states, decays, keeps, amount):
    size = states[0].shape[0]
    for k, state in enumerate(states):
        out[k * size : (k + 1) * size, :] = state
    row = iota((EXTRA, LANES), 0)
    extra = jnp.where(row == len(states), keeps, amount)
    for k, decay in enumerate(decays):
        extra = jnp.where(row == k, decay, extra)
    out[len(states) * size :, :] = extra


def carry_on(states, piece):
    return [jnp.exp(decay) * old + new for old, new, decay in zip(states, piece[0], piece[1])]


def add(first, second):
    return [one + other for one, other in zip(first, second)]


def total_kernel(*refs):
    pieces, out = refs[:GROUP], refs[-1]
    me = member_index()
    for v in range(GROUP):

        @pl.when(me == v)
        def _():
            members = [parts_of(piece) for piece in in_order(pieces, v)]
            states, decays, keeps, _ = members[0]
            for member in members[1:]:
                states = carry_on(states, member)
                decays = add(decays, member[1])
                keeps = keeps * member[2]
            amount = members[-1][3]
            for member in members[-2::-1]:
                amount = member[3] + member[2] * amount
            write_piece(out, states, decays, keeps, amount)


def round_kernel(bit, *refs):
    total, got, before, total_out, before_out = refs
    group = lax.axis_index("ctx") // GROUP
    mine, theirs, past = parts_of(total), parts_of(got), parts_of(before)
    decays, keeps = add(mine[1], theirs[1]), mine[2] * theirs[2]

    @pl.when(lax.rem(group // bit, 2) == 1)
    def _():
        write_piece(before_out, carry_on(theirs[0], past), add(past[1], theirs[1]), past[2], past[3])
        write_piece(total_out, carry_on(theirs[0], mine), decays, keeps, theirs[3] + theirs[2] * mine[3])

    @pl.when(lax.rem(group // bit, 2) == 0)
    def _():
        write_piece(before_out, past[0], past[1], past[2] * theirs[2], past[3] + past[2] * theirs[3])
        write_piece(total_out, carry_on(mine[0], theirs), decays, keeps, mine[3] + mine[2] * theirs[3])


def entering_kernel(bit, has_past, *refs):
    pieces, got = refs[:GROUP], refs[GROUP]
    past = refs[GROUP + 1] if has_past else None
    outs, carry_out, inside = refs[-GROUP - 2 : -2], refs[-2], refs[-1]
    near = refs[GROUP + 1 + has_past : GROUP + 8 + has_past]
    intra_groups(3, *near, inside)
    ctx = lax.axis_index("ctx")
    me = lax.rem(ctx, GROUP)
    is_later = lax.rem(ctx // GROUP // bit, 2) == 1
    theirs = parts_of(got)
    for v in range(GROUP):

        @pl.when(me == v)
        def _():
            members = [parts_of(piece) for piece in in_order(pieces, v)]
            arriving = [jnp.where(is_later, state, 0.0) for state in theirs[0]]
            amount = jnp.where(is_later, 0.0, theirs[3])
            if has_past:
                old = parts_of(past)
                arriving = carry_on(arriving, old)
                amount = old[3] + old[2] * amount
            size = arriving[0].shape[0]
            for m in range(GROUP):
                for k, state in enumerate(arriving):
                    outs[v ^ m][k * size : (k + 1) * size, :] = state
                if m < GROUP - 1:
                    arriving = carry_on(arriving, members[m])
            for m in range(GROUP - 1, v, -1):
                amount = members[m][3] + members[m][2] * amount
            carry_out[...] = jnp.broadcast_to(amount, carry_out.shape)


def readout_kernel(*refs):
    entering, (c_input, columns, inside, wide_row, out) = refs[:GROUP], refs[GROUP:]
    span, state = c_input.shape
    heads = wide_row.shape[1] // HEAD_DIM
    wide = wide_row.shape[1] // GROUP
    me = member_index()
    queries = c_input[...]
    by_token = columns[:, 128:]
    squares = jnp.zeros((span, 128), jnp.float32)
    values = jnp.zeros((span, 128), jnp.float32)
    for j in range(GROUP):
        part = lax.bitwise_xor(me, j)
        lanes = pl.ds(pl.multiple_of(part * wide, wide), wide)
        value = jnp.concatenate([entering[j][:state, :], entering[j][state:, :]], axis=1)
        high = value.astype(jnp.bfloat16)
        low = (value - high.astype(jnp.float32)).astype(jnp.bfloat16)
        carried = dot(queries, high) + dot(queries, low)
        decay = dot(by_token, selector(heads, 128, part * (heads // GROUP), wide))
        mixed = inside[:, lanes] + carried * decay
        readout = wide_row[0:1, lanes]
        squared, read = mixed * mixed, mixed * readout
        for k in range(0, wide, 128):
            squares = squares + squared[:, k : k + 128]
            values = values + read[:, k : k + 128]
    out[0:1, :] = jnp.sum(squares.T, axis=0, keepdims=True)
    out[1:2, :] = jnp.sum(values.T, axis=0, keepdims=True)


def last_kernel(channels, mine, other, suffix, carry, values_out, advantages_out, values, advantages, sems):
    sums = mine[...] + other[...]
    value = sums[1:2] / jnp.sqrt(sums[0:1] / channels + NORM_EPSILON)
    values[...] = value
    advantages[...] = suffix[0:1, :] + suffix[1:2, :] * carry[0:1, 0:1] - value
    copies = [
        pltpu.make_async_copy(values, values_out, sems.at[0]),
        pltpu.make_async_copy(advantages, advantages_out, sems.at[1]),
    ]
    for copy in copies:
        copy.start()
    for copy in copies:
        copy.wait()


def call(kernel, shapes, name, *args, hbm_in=False, hbm_out=False, scratch=(), aliases=None):
    near, far = pl.BlockSpec(memory_space=pltpu.VMEM), pl.BlockSpec(memory_space=pltpu.HBM)
    if hbm_in:
        args = [pltpu.with_memory_space_constraint(arg, pltpu.HBM) for arg in args]
    return pl.pallas_call(
        kernel,
        out_shape=[jax.ShapeDtypeStruct(*shape) for shape in shapes],
        in_specs=[far if hbm_in else near] * len(args),
        out_specs=[far if hbm_out else near] * len(shapes),
        scratch_shapes=scratch,
        input_output_aliases=aliases or {},
        compiler_params=pltpu.CompilerParams(vmem_limit_bytes=VMEM_BYTES),
        name=name,
    )(*args)


def swap(value, axis, mask):
    count = lax.axis_size(axis)
    return lax.ppermute(value, axis, [(k, k ^ mask) for k in range(count)])


def local(
    features,
    b_input,
    c_input,
    step_input,
    decay_log,
    skip_gain,
    norm_gain,
    value_weight,
    rewards,
    reward_keep_mask,
    episode_end,
):
    span, width = features.shape
    heads = step_input.shape[0]
    state = b_input.shape[1]
    halves = width // GROUP // LANES
    count = lax.axis_size("ctx")
    groups = count // GROUP
    assert span == SPAN and count == groups * GROUP and groups > 1 and groups & (groups - 1) == 0 and halves == 2
    f32, bf16, i32 = jnp.float32, jnp.bfloat16, jnp.int32
    piece = ((halves * state + EXTRA, LANES), f32)
    states = ((halves * state, LANES), f32)
    columns_shape, wide_shape, inside_shape = ((span, 256), bf16), ((2, width), f32), ((span, width), f32)

    made = call(
        state_kernel,
        [piece] * GROUP
        + [
            ((span, width), bf16),
            ((span, state), bf16),
            ((span, state), bf16),
            ((heads, span), f32),
            ((heads, span), f32),
            ((8, span), f32),
            ((1, heads), f32),
            ((1, width), f32),
            ((1, width), f32),
            columns_shape,
            wide_shape,
            inside_shape,
        ],
        "block_states",
        step_input,
        decay_log[None, :],
        rewards[None, :],
        reward_keep_mask[None, :],
        episode_end[None, :],
        features,
        b_input,
        c_input,
        skip_gain[None, :],
        norm_gain[None, :],
        value_weight[None, :],
        hbm_in=True,
        scratch=[
            pltpu.VMEM((heads, span), f32),
            pltpu.VMEM((1, heads), f32),
            pltpu.VMEM((1, span), f32),
            pltpu.VMEM((1, span), i32),
            pltpu.VMEM((1, span), i32),
            pltpu.SemaphoreType.DMA((11,)),
        ],
    )
    pieces, made = made[:GROUP], made[GROUP:]
    got = [pieces[0]] + [swap(pieces[j], "ctx", j) for j in range(1, GROUP)]
    columns, wide_row, inside, suffix = call(
        first_kernel,
        [columns_shape, wide_shape, inside_shape, ((8, span), f32)],
        "inside_first",
        *made,
        aliases={9: 0, 10: 1, 11: 2},
    )
    near = (*made[:5], columns, wide_row)
    queries = made[2]
    (total,) = call(total_kernel, [piece], "group_total", *got, suffix)
    past = None
    bit = 1
    while bit * 2 < groups:
        other = swap(total, "ctx", GROUP * bit)
        if past is None:
            row = jnp.arange(piece[0][0])[:, None]
            past = jnp.where(row == halves * (state + 1), 1.0, 0.0).astype(f32) * jnp.ones((1, LANES), f32)
        total, past = call(
            functools.partial(round_kernel, bit), [piece, piece], "scan_round", total, other, past
        )
        bit *= 2
    other = swap(total, "ctx", GROUP * bit)
    (inside,) = call(second_kernel, [inside_shape], "inside_second", *near, inside, aliases={len(near): 0})
    operands = (*got, other, *([] if past is None else [past]), *near, inside)
    made = call(
        functools.partial(entering_kernel, bit, past is not None),
        [states] * GROUP + [((8, LANES), f32), inside_shape],
        "entering_states",
        *operands,
        aliases={len(operands) - 1: GROUP + 1},
    )
    entering, carry, inside = made[:GROUP], made[GROUP], made[GROUP + 1]
    arrived = [entering[0]] + [swap(entering[j], "ctx", j) for j in range(1, GROUP)]
    (sums,) = call(readout_kernel, [((2, span), f32)], "readout", *arrived, queries, columns, inside, wide_row)
    values, advantages = call(
        functools.partial(last_kernel, width * lax.axis_size("head")),
        [((1, span), f32)] * 2,
        "values_and_advantages",
        sums,
        swap(sums, "head", 1),
        suffix,
        carry,
        hbm_out=True,
        scratch=[pltpu.VMEM((1, span), f32), pltpu.VMEM((1, span), f32), pltpu.SemaphoreType.DMA((2,))],
    )
    return (values[0], advantages[0])


def solution(mesh):
    placed = (
        P(("traj", "ctx"), "head"),
        P(("traj", "ctx"), None),
        P(("traj", "ctx"), None),
        P("head", ("traj", "ctx")),
        P("head"),
        P("head"),
        P("head"),
        P("head"),
        P(("traj", "ctx")),
        P(("traj", "ctx")),
        P(("traj", "ctx")),
    )
    return jax.shard_map(
        local,
        mesh=mesh,
        in_specs=placed,
        out_specs=(P(("traj", "ctx")), P(("traj", "ctx"))),
        check_vma=False,
    )
```

```python
import functools

import jax
import jax.numpy as jnp
from jax import lax
from jax.experimental import pallas as pl
from jax.experimental.pallas import tpu as pltpu
from jax.sharding import PartitionSpec as P

HEAD_DIM = 32
SPAN = 256
GROUP = 4
LANES = 128
LATE = 0
FIRST_ORDERS = ((0, 1, 2, 3), (0, 2, 1, 3))
LAST_ORDERS = ((0, 3, 1, 2), (0, 1, 2, 3))
SHARES = ((0, 2, 4, 8), (0, 0, 4, 8))
EXTRA = 8
NORM_EPSILON = 1e-05
VMEM_BYTES = 24 * 1024 * 1024


def split3(value):
    high = value.astype(jnp.bfloat16).astype(jnp.float32)
    rest = value - high
    middle = rest.astype(jnp.bfloat16).astype(jnp.float32)
    return high, middle, (rest - middle).astype(jnp.bfloat16).astype(jnp.float32)


def dot(a, b, contract=((1,), (0,))):
    return lax.dot_general(a, b, (contract, ((), ())), preferred_element_type=jnp.float32)


def iota(shape, dim):
    return lax.broadcasted_iota(jnp.int32, shape, dim)


def column(row):
    n = row.shape[1]
    return jnp.sum(jnp.where(iota((n, n), 0) == iota((n, n), 1), row, 0.0), axis=1, keepdims=True)


def over_channels(per_head, first_head, channels):
    heads = per_head.shape[0]
    match = iota((heads, channels), 0) == first_head + iota((heads, channels), 1) // HEAD_DIM
    return jnp.sum(jnp.where(match, per_head, 0.0), axis=0, keepdims=True)


def selector(heads, rows, first_head, channels):
    row = iota((rows, channels), 0)
    match = (lax.rem(row, heads) == first_head + iota((rows, channels), 1) // HEAD_DIM) & (row < 3 * heads)
    return jnp.where(match, 1.0, 0.0).astype(jnp.bfloat16)


def is_late():
    return lax.axis_index("head") == LATE


def member_index():
    return lax.rem(lax.axis_index("ctx"), GROUP)


def partner_index(orders, slot):
    return lax.bitwise_xor(member_index(), jnp.where(lax.axis_index("head") == 0, orders[0][slot], orders[1][slot]))


def each_place(body):
    for core in range(len(FIRST_ORDERS)):
        for v in range(GROUP):

            @pl.when((member_index() == v) & (lax.axis_index("head") == core))
            def _():
                body(v, *([orders[core].index(v ^ m) for m in range(GROUP)] for orders in (FIRST_ORDERS, LAST_ORDERS)))


def prepare(cum_ref, skip, norm, weight, columns_out, wide_out):
    heads, span = cum_ref.shape
    cum = cum_ref[...]
    pad = jnp.zeros((128 - 3 * heads, span), jnp.float32)
    columns_out[:, :128] = jnp.concatenate(split3(cum) + (jnp.ones_like(pad),), axis=0).T.astype(jnp.bfloat16)
    columns_out[:, 128:] = jnp.concatenate(split3(jnp.exp(cum)) + (pad,), axis=0).T.astype(jnp.bfloat16)
    wide_out[0:1, :] = norm[...] * weight[...]
    wide_out[1:2, :] = over_channels(column(skip[...]), 0, heads * HEAD_DIM)


def state_kernel(*refs):
    sources, refs = refs[:11], refs[11:]
    pieces, refs = refs[:GROUP], refs[GROUP:]
    features, b_input, c_input, cum_out, step_out, rows, skip, norm, weight, columns, wide_row, inside = refs[:12]
    step_in, decay_log, rewards, keep, ends, sems = refs[12:]
    targets = (step_in, decay_log, rewards, keep, ends, features, b_input, c_input, skip, norm, weight)
    copies = [pltpu.make_async_copy(src, dst, sems.at[i]) for i, (src, dst) in enumerate(zip(sources, targets))]
    for copy in copies:
        copy.start()
    heads, span = step_in.shape
    state = b_input.shape[1]
    wide = features.shape[1] // GROUP
    for copy in copies[:5]:
        copy.wait()
    raw = step_in[...]
    step = jnp.maximum(raw, 0.0) + jnp.log1p(jnp.exp(-jnp.abs(raw)))
    log_decay = -jnp.exp(column(decay_log[...])) * step
    ends_row = ends[...].astype(jnp.float32)
    live = keep[...].astype(jnp.float32) * rewards[...]
    upper = jnp.where(iota((span, span), 0) <= iota((span, span), 1), 1.0, 0.0).astype(jnp.bfloat16)
    stacked = jnp.concatenate(split3(log_decay) + (jnp.broadcast_to(ends_row, (16, span)),), axis=0)
    summed = dot(stacked.astype(jnp.bfloat16), upper)
    cum = summed[:heads] + summed[heads : 2 * heads] + summed[2 * heads : 3 * heads]
    through = summed[3 * heads : 3 * heads + 1]
    before = through - ends_row
    total = cum[:, span - 1 :]
    first_sum = jnp.sum(jnp.where(before == 0.0, live, 0.0), axis=1, keepdims=True)
    still_open = jnp.where(through[:, span - 1 :] == 0.0, 1.0, 0.0)
    coefficient = jnp.exp(total - cum) * step
    pad = jnp.zeros((128 - 3 * heads, span), jnp.float32)
    by_token = jnp.concatenate(split3(coefficient) + (pad,), axis=0).T.astype(jnp.bfloat16)
    cum_out[...] = cum
    step_out[...] = step
    rows[...] = jnp.concatenate([live, through, before, jnp.zeros((5, span), jnp.float32)], axis=0)
    for copy in copies[5:]:
        copy.wait()

    @pl.when(is_late())
    def _():
        prepare(cum_out, skip, norm, weight, columns, wide_row)
        intra_groups(0, features, b_input, c_input, cum_out, step_out, columns, wide_row, inside)

    keys = b_input[...].T
    row = iota((EXTRA, LANES), 0)
    for j in (1, 2, 3, 0):
        part = partner_index(FIRST_ORDERS, j)
        first_head = part * (heads // GROUP)
        feat = features[:, pl.ds(pl.multiple_of(part * wide, wide), wide)]
        spread = dot(by_token, selector(heads, 128, first_head, wide))
        scaled = (spread * feat.astype(jnp.float32)).astype(jnp.bfloat16)
        states = dot(keys, scaled)
        decay = over_channels(total, first_head, wide)
        extra = jnp.where(row == wide // LANES, still_open, first_sum)
        for k in range(wide // LANES):
            pieces[j][k * state : (k + 1) * state, :] = states[:, k * LANES : (k + 1) * LANES]
            extra = jnp.where(row == k, decay[:, k * LANES : (k + 1) * LANES], extra)
        pieces[j][wide // LANES * state :, :] = extra


def intra_groups(stage, features, b_input, c_input, cum_ref, step_ref, columns, wide_row, out):
    start, stop = (jnp.where(is_late(), SHARES[0][k], SHARES[1][k]) for k in (stage, stage + 1))
    heads, span = cum_ref.shape
    at_once = 128 // HEAD_DIM
    t, s = iota((span, span), 0), iota((span, span), 1)
    scores = jnp.where(t >= s, dot(c_input[...], b_input[...], ((1,), (1,))), 0.0)
    by_token = columns[:, :128]
    row = iota((128, span), 0)

    def some_heads(index, carry):
        first = index * at_once
        lanes = pl.ds(pl.multiple_of(index * 128, 128), 128)
        feat = features[:, lanes]
        total = feat.astype(jnp.float32) * wide_row[1:2, lanes]
        owner = iota((span, 128), 1) // HEAD_DIM
        for j in range(at_once):
            head = first + j
            cum = cum_ref[pl.ds(head, 1), :]
            high, middle, low = split3(cum)
            other = jnp.where(
                row < 3 * heads,
                jnp.where(lax.rem(row, heads) == head, 1.0, 0.0),
                jnp.where(
                    row == 3 * heads,
                    -high,
                    jnp.where(row == 3 * heads + 1, -middle, jnp.where(row == 3 * heads + 2, -low, 0.0)),
                ),
            ).astype(jnp.bfloat16)
            gap = jnp.minimum(dot(by_token, other), 0.0)
            weights = (scores * jnp.exp(gap) * step_ref[pl.ds(head, 1), :]).astype(jnp.bfloat16)
            total = total + dot(weights, jnp.where(owner == j, feat, jnp.zeros_like(feat)))
        out[:, lanes] = total
        return carry

    lax.fori_loop(start, stop, some_heads, 0)


def first_kernel(
    features, b_input, c_input, cum_ref, step_ref, rows, skip, norm, weight, _0, _1, _2, columns, wide_row, out, suffix
):
    @pl.when(jnp.logical_not(is_late()))
    def _():
        prepare(cum_ref, skip, norm, weight, columns, wide_row)

    intra_groups(1, features, b_input, c_input, cum_ref, step_ref, columns, wide_row, out)

    span = cum_ref.shape[1]
    t, s = iota((span, span), 0), iota((span, span), 1)
    live, through, before = rows[0:1, :], rows[1:2, :], rows[2:3, :]
    reach = jnp.where((t >= s) & (column(before) == before), column(live), 0.0)
    sums = jnp.sum(reach, axis=0, keepdims=True)
    open_end = jnp.where(before == through[:, span - 1 :], 1.0, 0.0)
    suffix[...] = jnp.concatenate([sums, open_end, jnp.zeros((6, span), jnp.float32)], axis=0)


def second_kernel(features, b_input, c_input, cum_ref, step_ref, columns, wide_row, _, out):
    intra_groups(2, features, b_input, c_input, cum_ref, step_ref, columns, wide_row, out)


def parts_of(piece):
    halves = 2
    size = (piece.shape[0] - EXTRA) // halves
    extra = piece[halves * size :, :]
    return (
        [piece[k * size : (k + 1) * size, :] for k in range(halves)],
        [extra[k : k + 1] for k in range(halves)],
        extra[halves : halves + 1],
        extra[halves + 1 : halves + 2],
    )


def write_piece(out, states, decays, keeps, amount):
    size = states[0].shape[0]
    for k, state in enumerate(states):
        out[k * size : (k + 1) * size, :] = state
    row = iota((EXTRA, LANES), 0)
    extra = jnp.where(row == len(states), keeps, amount)
    for k, decay in enumerate(decays):
        extra = jnp.where(row == k, decay, extra)
    out[len(states) * size :, :] = extra


def carry_on(states, piece):
    return [jnp.exp(decay) * old + new for old, new, decay in zip(states, piece[0], piece[1])]


def add(first, second):
    return [one + other for one, other in zip(first, second)]


def total_kernel(*refs):
    pieces, out = refs[:GROUP], refs[-1]

    @each_place
    def _(me, first, last):
        members = [parts_of(pieces[slot]) for slot in first]
        states, decays, keeps, _ = members[0]
        for member in members[1:]:
            states = carry_on(states, member)
            decays = add(decays, member[1])
            keeps = keeps * member[2]
        amount = members[-1][3]
        for member in members[-2::-1]:
            amount = member[3] + member[2] * amount
        write_piece(out, states, decays, keeps, amount)


def round_kernel(bit, *refs):
    total, got, before, total_out, before_out = refs
    group = lax.axis_index("ctx") // GROUP
    mine, theirs, past = parts_of(total), parts_of(got), parts_of(before)
    decays, keeps = add(mine[1], theirs[1]), mine[2] * theirs[2]

    @pl.when(lax.rem(group // bit, 2) == 1)
    def _():
        write_piece(before_out, carry_on(theirs[0], past), add(past[1], theirs[1]), past[2], past[3])
        write_piece(total_out, carry_on(theirs[0], mine), decays, keeps, theirs[3] + theirs[2] * mine[3])

    @pl.when(lax.rem(group // bit, 2) == 0)
    def _():
        write_piece(before_out, past[0], past[1], past[2] * theirs[2], past[3] + past[2] * theirs[3])
        write_piece(total_out, carry_on(mine[0], theirs), decays, keeps, mine[3] + mine[2] * theirs[3])


def entering_kernel(bit, has_got, has_past, *refs):
    pieces, refs = refs[:GROUP], refs[GROUP:]
    got, refs = (refs[0], refs[1:]) if has_got else (None, refs)
    past, refs = (refs[0], refs[1:]) if has_past else (None, refs)
    outs, carry_out = refs[-GROUP - 1 : -1], refs[-1]
    is_later = lax.rem(lax.axis_index("ctx") // GROUP // bit, 2) == 1

    @each_place
    def _(me, first, last):
        members = [parts_of(pieces[slot]) for slot in first]
        size = members[0][0][0].shape
        arriving = [jnp.zeros(size, jnp.float32)] * 2
        keeps, amount = jnp.ones((1, LANES), jnp.float32), jnp.zeros((1, LANES), jnp.float32)
        if has_got:
            theirs = parts_of(got)
            arriving = [jnp.where(is_later, state, 0.0) for state in theirs[0]]
            keeps = jnp.where(is_later, keeps, theirs[2])
            amount = jnp.where(is_later, amount, theirs[3])
        if has_past:
            old = parts_of(past)
            arriving = carry_on(arriving, old)
            amount = old[3] + old[2] * amount
        for m in range(GROUP):
            for k, state in enumerate(arriving):
                outs[last[m]][k * size[0] : (k + 1) * size[0], :] = state
            if m < GROUP - 1:
                arriving = carry_on(arriving, members[m])
        for m in range(GROUP - 1, me, -1):
            amount = members[m][3] + members[m][2] * amount
            keeps = keeps * members[m][2]
        row = iota(carry_out.shape, 0)
        carry_out[...] = jnp.where(row == 0, amount, keeps)


def readout_kernel(*refs):
    entering, (c_input, columns, inside, wide_row, out) = refs[:GROUP], refs[GROUP:]
    span, state = c_input.shape
    heads = wide_row.shape[1] // HEAD_DIM
    wide = wide_row.shape[1] // GROUP
    queries = c_input[...]
    by_token = columns[:, 128:]
    squares = jnp.zeros((span, 128), jnp.float32)
    values = jnp.zeros((span, 128), jnp.float32)
    for j in range(GROUP):
        part = partner_index(LAST_ORDERS, j)
        lanes = pl.ds(pl.multiple_of(part * wide, wide), wide)
        value = jnp.concatenate([entering[j][:state, :], entering[j][state:, :]], axis=1)
        high = value.astype(jnp.bfloat16)
        low = (value - high.astype(jnp.float32)).astype(jnp.bfloat16)
        carried = dot(queries, high) + dot(queries, low)
        decay = dot(by_token, selector(heads, 128, part * (heads // GROUP), wide))
        mixed = inside[:, lanes] + carried * decay
        readout = wide_row[0:1, lanes]
        squared, read = mixed * mixed, mixed * readout
        for k in range(0, wide, 128):
            squares = squares + squared[:, k : k + 128]
            values = values + read[:, k : k + 128]
    out[0:1, :] = jnp.sum(squares.T, axis=0, keepdims=True)
    out[1:2, :] = jnp.sum(values.T, axis=0, keepdims=True)


def last_kernel(channels, first_group_early, mine, other, suffix, carry, got, values_out, advantages_out, values, advantages, sems):
    sums = mine[...] + other[...]
    value = sums[1:2] / jnp.sqrt(sums[0:1] / channels + NORM_EPSILON)
    values[...] = value
    amount = carry[0:1, 0:1]
    if first_group_early:
        later = jnp.where(lax.axis_index("ctx") < GROUP, parts_of(got)[3][:, 0:1], 0.0)
        amount = amount + carry[1:2, 0:1] * later
    advantages[...] = suffix[0:1, :] + suffix[1:2, :] * amount - value
    copies = [
        pltpu.make_async_copy(values, values_out, sems.at[0]),
        pltpu.make_async_copy(advantages, advantages_out, sems.at[1]),
    ]
    for copy in copies:
        copy.start()
    for copy in copies:
        copy.wait()


def call(kernel, shapes, name, *args, hbm_in=False, hbm_out=False, scratch=(), aliases=None):
    near, far = pl.BlockSpec(memory_space=pltpu.VMEM), pl.BlockSpec(memory_space=pltpu.HBM)
    if hbm_in:
        args = [pltpu.with_memory_space_constraint(arg, pltpu.HBM) for arg in args]
    return pl.pallas_call(
        kernel,
        out_shape=[jax.ShapeDtypeStruct(*shape) for shape in shapes],
        in_specs=[far if hbm_in else near] * len(args),
        out_specs=[far if hbm_out else near] * len(shapes),
        scratch_shapes=scratch,
        input_output_aliases=aliases or {},
        compiler_params=pltpu.CompilerParams(vmem_limit_bytes=VMEM_BYTES),
        name=name,
    )(*args)


def swap(value, axis, mask):
    count = lax.axis_size(axis)
    return lax.ppermute(value, axis, [(k, k ^ mask) for k in range(count)])


def swap_slots(orders, pieces):
    cores = lax.axis_size("head")
    assert cores == len(orders)
    pairs = [
        [(k * cores + core, (k ^ orders[core][slot]) * cores + core) for k in range(lax.axis_size("ctx")) for core in range(cores)]
        for slot in range(1, GROUP)
    ]
    return [pieces[0]] + [lax.ppermute(piece, ("ctx", "head"), pair) for piece, pair in zip(pieces[1:], pairs)]


def local(
    features,
    b_input,
    c_input,
    step_input,
    decay_log,
    skip_gain,
    norm_gain,
    value_weight,
    rewards,
    reward_keep_mask,
    episode_end,
):
    span, width = features.shape
    heads = step_input.shape[0]
    state = b_input.shape[1]
    halves = width // GROUP // LANES
    count = lax.axis_size("ctx")
    groups = count // GROUP
    assert span == SPAN and count == groups * GROUP and groups > 1 and groups & (groups - 1) == 0 and halves == 2
    f32, bf16, i32 = jnp.float32, jnp.bfloat16, jnp.int32
    piece = ((halves * state + EXTRA, LANES), f32)
    states = ((halves * state, LANES), f32)
    columns_shape, wide_shape, inside_shape = ((span, 256), bf16), ((2, width), f32), ((span, width), f32)

    made = call(
        state_kernel,
        [piece] * GROUP
        + [
            ((span, width), bf16),
            ((span, state), bf16),
            ((span, state), bf16),
            ((heads, span), f32),
            ((heads, span), f32),
            ((8, span), f32),
            ((1, heads), f32),
            ((1, width), f32),
            ((1, width), f32),
            columns_shape,
            wide_shape,
            inside_shape,
        ],
        "block_states",
        step_input,
        decay_log[None, :],
        rewards[None, :],
        reward_keep_mask[None, :],
        episode_end[None, :],
        features,
        b_input,
        c_input,
        skip_gain[None, :],
        norm_gain[None, :],
        value_weight[None, :],
        hbm_in=True,
        scratch=[
            pltpu.VMEM((heads, span), f32),
            pltpu.VMEM((1, heads), f32),
            pltpu.VMEM((1, span), f32),
            pltpu.VMEM((1, span), i32),
            pltpu.VMEM((1, span), i32),
            pltpu.SemaphoreType.DMA((11,)),
        ],
    )
    pieces, made = made[:GROUP], made[GROUP:]
    got = swap_slots(FIRST_ORDERS, pieces)
    columns, wide_row, inside, suffix = call(
        first_kernel,
        [columns_shape, wide_shape, inside_shape, ((8, span), f32)],
        "inside_first",
        *made,
        aliases={9: 0, 10: 1, 11: 2},
    )
    near = (*made[:5], columns, wide_row)
    queries = made[2]
    (total,) = call(total_kernel, [piece], "group_total", *got, suffix)
    past = None
    bit = 1
    while bit * 2 < groups:
        other = swap(total, "ctx", GROUP * bit)
        if past is None:
            row = jnp.arange(piece[0][0])[:, None]
            past = jnp.where(row == halves * (state + 1), 1.0, 0.0).astype(f32) * jnp.ones((1, LANES), f32)
        total, past = call(
            functools.partial(round_kernel, bit), [piece, piece], "scan_round", total, other, past
        )
        bit *= 2
    other = swap(total, "ctx", GROUP * bit)
    (inside,) = call(second_kernel, [inside_shape], "inside_second", *near, inside, aliases={len(near): 0})

    def finish(has_got):
        operands = (*got, *([other] if has_got else []), *([] if past is None else [past]))
        made = call(
            functools.partial(entering_kernel, bit, has_got, past is not None),
            [states] * GROUP + [((8, LANES), f32)],
            "entering_states",
            *operands,
            *([] if past is None else [inside]),
        )
        arrived = swap_slots(LAST_ORDERS, made[:GROUP])
        (sums,) = call(readout_kernel, [((2, span), f32)], "readout", *arrived, queries, columns, inside, wide_row)
        return sums, made[GROUP]

    first_group_early = groups == 2
    if first_group_early:
        is_first = lax.axis_index("ctx") < GROUP
        nothing = lambda: (jnp.zeros((2, span), f32), jnp.zeros((8, LANES), f32))
        early = lax.cond(is_first, lambda: finish(False), nothing)
        sums, carry = lax.cond(is_first, lambda: early, lambda: finish(True))
    else:
        sums, carry = finish(True)
    values, advantages = call(
        functools.partial(last_kernel, width * lax.axis_size("head"), first_group_early),
        [((1, span), f32)] * 2,
        "values_and_advantages",
        sums,
        swap(sums, "head", 1),
        suffix,
        carry,
        other,
        hbm_out=True,
        scratch=[pltpu.VMEM((1, span), f32), pltpu.VMEM((1, span), f32), pltpu.SemaphoreType.DMA((2,))],
    )
    return (values[0], advantages[0])


def solution(mesh):
    placed = (
        P(("traj", "ctx"), "head"),
        P(("traj", "ctx"), None),
        P(("traj", "ctx"), None),
        P("head", ("traj", "ctx")),
        P("head"),
        P("head"),
        P("head"),
        P("head"),
        P(("traj", "ctx")),
        P(("traj", "ctx")),
        P(("traj", "ctx")),
    )
    return jax.shard_map(
        local,
        mesh=mesh,
        in_specs=placed,
        out_specs=(P(("traj", "ctx")), P(("traj", "ctx"))),
        check_vma=False,
    )
```

```python
import functools

import jax
import jax.numpy as jnp
from jax import lax
from jax.experimental import pallas as pl
from jax.experimental.pallas import tpu as pltpu
from jax.sharding import PartitionSpec as P

HEAD_DIM = 32
SPAN = 256
GROUP = 4
LANES = 128
FIRST_ORDERS = ((0, 1, 2, 3), (0, 2, 1, 3))
EARLY_ORDERS = ((0, 3, 1, 2), (0, 1, 2, 3))
LAST_ORDERS = ((0, 3, 1, 2), (0, 1, 2, 3))
READOUTS = ((0, 1, 2, 3),)
SHARES = (((0, 1, 4, 8), (0, 0, 7, 8)), ((0, 1, 6, 8), (0, 0, 6, 8)))
EXTRA = 8
NORM_EPSILON = 1e-05
VMEM_BYTES = 24 * 1024 * 1024


def split3(value):
    high = value.astype(jnp.bfloat16).astype(jnp.float32)
    rest = value - high
    middle = rest.astype(jnp.bfloat16).astype(jnp.float32)
    return high, middle, (rest - middle).astype(jnp.bfloat16).astype(jnp.float32)


def dot(a, b, contract=((1,), (0,))):
    return lax.dot_general(a, b, (contract, ((), ())), preferred_element_type=jnp.float32)


def iota(shape, dim):
    return lax.broadcasted_iota(jnp.int32, shape, dim)


def column(row):
    n = row.shape[1]
    return jnp.sum(jnp.where(iota((n, n), 0) == iota((n, n), 1), row, 0.0), axis=1, keepdims=True)


def over_channels(per_head, first_head, channels):
    heads = per_head.shape[0]
    match = iota((heads, channels), 0) == first_head + iota((heads, channels), 1) // HEAD_DIM
    return jnp.sum(jnp.where(match, per_head, 0.0), axis=0, keepdims=True)


def selector(heads, rows, first_head, channels):
    row = iota((rows, channels), 0)
    match = (lax.rem(row, heads) == first_head + iota((rows, channels), 1) // HEAD_DIM) & (row < 3 * heads)
    return jnp.where(match, 1.0, 0.0).astype(jnp.bfloat16)


def member_index():
    return lax.rem(lax.axis_index("ctx"), GROUP)


def partner_index(orders, slot):
    return lax.bitwise_xor(member_index(), jnp.where(lax.axis_index("head") == 0, orders[0][slot], orders[1][slot]))


def each_place(last_orders, body):
    for core in range(len(FIRST_ORDERS)):
        for v in range(GROUP):

            @pl.when((member_index() == v) & (lax.axis_index("head") == core))
            def _():
                body(v, *([orders[core].index(v ^ m) for m in range(GROUP)] for orders in (FIRST_ORDERS, last_orders)))


def prepare(cum_ref, skip, norm, weight, columns_out, wide_out):
    heads, span = cum_ref.shape
    cum = cum_ref[...]
    pad = jnp.zeros((128 - 3 * heads, span), jnp.float32)
    columns_out[:, :128] = jnp.concatenate(split3(cum) + (jnp.ones_like(pad),), axis=0).T.astype(jnp.bfloat16)
    columns_out[:, 128:] = jnp.concatenate(split3(jnp.exp(cum)) + (pad,), axis=0).T.astype(jnp.bfloat16)
    wide_out[0:1, :] = norm[...] * weight[...]
    wide_out[1:2, :] = over_channels(column(skip[...]), 0, heads * HEAD_DIM)


def write_pieces(slots, token, features, b_input, total, still_open, first_sum, outs):
    keys = b_input[...].T
    state = keys.shape[0]
    heads = total.shape[0]
    wide = features.shape[1] // GROUP
    row = iota((EXTRA, LANES), 0)
    by_token = token[...].astype(jnp.bfloat16)
    for slot, out in zip(slots, outs):
        part = partner_index(FIRST_ORDERS, slot)
        first_head = part * (heads // GROUP)
        feat = features[:, pl.ds(pl.multiple_of(part * wide, wide), wide)]
        spread = dot(by_token, selector(heads, 128, first_head, wide))
        scaled = (spread * feat.astype(jnp.float32)).astype(jnp.bfloat16)
        states = dot(keys, scaled)
        decay = over_channels(total, first_head, wide)
        extra = jnp.where(row == wide // LANES, still_open, first_sum)
        for k in range(wide // LANES):
            out[k * state : (k + 1) * state, :] = states[:, k * LANES : (k + 1) * LANES]
            extra = jnp.where(row == k, decay[:, k * LANES : (k + 1) * LANES], extra)
        out[wide // LANES * state :, :] = extra


def state_kernel(*refs):
    sources, refs = refs[:11], refs[11:]
    pieces, refs = refs[: GROUP - 1], refs[GROUP - 1 :]
    features, b_input, c_input, cum_out, step_out, rows, skip, norm, weight, token, columns, wide_row, inside = refs[:13]
    step_in, decay_log, rewards, keep, ends, sems = refs[13:]
    targets = (step_in, decay_log, rewards, keep, ends, features, b_input, c_input, skip, norm, weight)
    copies = [pltpu.make_async_copy(src, dst, sems.at[i]) for i, (src, dst) in enumerate(zip(sources, targets))]
    for copy in copies:
        copy.start()
    heads, span = step_in.shape
    for copy in copies[:5]:
        copy.wait()
    raw = step_in[...]
    step = jnp.maximum(raw, 0.0) + jnp.log1p(jnp.exp(-jnp.abs(raw)))
    log_decay = -jnp.exp(column(decay_log[...])) * step
    ends_row = ends[...].astype(jnp.float32)
    live = keep[...].astype(jnp.float32) * rewards[...]
    upper = jnp.where(iota((span, span), 0) <= iota((span, span), 1), 1.0, 0.0).astype(jnp.bfloat16)
    stacked = jnp.concatenate(split3(log_decay) + (jnp.broadcast_to(ends_row, (16, span)),), axis=0)
    summed = dot(stacked.astype(jnp.bfloat16), upper)
    cum = summed[:heads] + summed[heads : 2 * heads] + summed[2 * heads : 3 * heads]
    through = summed[3 * heads : 3 * heads + 1]
    before = through - ends_row
    total = cum[:, span - 1 :]
    first_sum = jnp.sum(jnp.where(before == 0.0, live, 0.0), axis=1, keepdims=True)
    still_open = jnp.where(through[:, span - 1 :] == 0.0, 1.0, 0.0)
    coefficient = jnp.exp(total - cum) * step
    pad = jnp.zeros((128 - 3 * heads, span), jnp.float32)
    token[...] = jnp.concatenate(split3(coefficient) + (pad,), axis=0).T
    cum_out[...] = cum
    step_out[...] = step
    flags = [jnp.broadcast_to(value, (1, span)) for value in (still_open, first_sum)]
    rows[...] = jnp.concatenate([live, through, before, *flags, jnp.zeros((3, span), jnp.float32)], axis=0)
    for copy in copies[5:]:
        copy.wait()

    @pl.when(share_bound(1) > 0)
    def _():
        prepare(cum_out, skip, norm, weight, columns, wide_row)
        intra_groups(0, features, b_input, c_input, cum_out, step_out, columns, wide_row, inside)

    write_pieces((1, 2, 3), token, features, b_input, total, still_open, first_sum, pieces)


def share_bound(k):
    first_group, first_core = lax.axis_index("ctx") < GROUP, lax.axis_index("head") == 0
    return jnp.where(
        first_group,
        jnp.where(first_core, SHARES[0][0][k], SHARES[0][1][k]),
        jnp.where(first_core, SHARES[1][0][k], SHARES[1][1][k]),
    )


def intra_groups(stage, features, b_input, c_input, cum_ref, step_ref, columns, wide_row, out):
    start, stop = share_bound(stage), share_bound(stage + 1)
    heads, span = cum_ref.shape
    at_once = 128 // HEAD_DIM
    t, s = iota((span, span), 0), iota((span, span), 1)
    scores = jnp.where(t >= s, dot(c_input[...], b_input[...], ((1,), (1,))), 0.0)
    by_token = columns[:, :128]
    row = iota((128, span), 0)

    def some_heads(index, carry):
        first = index * at_once
        lanes = pl.ds(pl.multiple_of(index * 128, 128), 128)
        feat = features[:, lanes]
        total = feat.astype(jnp.float32) * wide_row[1:2, lanes]
        owner = iota((span, 128), 1) // HEAD_DIM
        for j in range(at_once):
            head = first + j
            cum = cum_ref[pl.ds(head, 1), :]
            high, middle, low = split3(cum)
            other = jnp.where(
                row < 3 * heads,
                jnp.where(lax.rem(row, heads) == head, 1.0, 0.0),
                jnp.where(
                    row == 3 * heads,
                    -high,
                    jnp.where(row == 3 * heads + 1, -middle, jnp.where(row == 3 * heads + 2, -low, 0.0)),
                ),
            ).astype(jnp.bfloat16)
            gap = jnp.minimum(dot(by_token, other), 0.0)
            weights = (scores * jnp.exp(gap) * step_ref[pl.ds(head, 1), :]).astype(jnp.bfloat16)
            total = total + dot(weights, jnp.where(owner == j, feat, jnp.zeros_like(feat)))
        out[:, lanes] = total
        return carry

    lax.fori_loop(start, stop, some_heads, 0)


def first_kernel(
    features,
    b_input,
    c_input,
    cum_ref,
    step_ref,
    rows,
    skip,
    norm,
    weight,
    token,
    _0,
    _1,
    _2,
    columns,
    wide_row,
    out,
    suffix,
    own_piece,
):
    span = cum_ref.shape[1]
    write_pieces(
        (0,), token, features, b_input, cum_ref[:, span - 1 :], rows[3:4, 0:1], rows[4:5, 0:1], (own_piece,)
    )

    @pl.when(share_bound(1) == 0)
    def _():
        prepare(cum_ref, skip, norm, weight, columns, wide_row)

    intra_groups(1, features, b_input, c_input, cum_ref, step_ref, columns, wide_row, out)

    t, s = iota((span, span), 0), iota((span, span), 1)
    live, through, before = rows[0:1, :], rows[1:2, :], rows[2:3, :]
    reach = jnp.where((t >= s) & (column(before) == before), column(live), 0.0)
    sums = jnp.sum(reach, axis=0, keepdims=True)
    open_end = jnp.where(before == through[:, span - 1 :], 1.0, 0.0)
    suffix[...] = jnp.concatenate([sums, open_end, jnp.zeros((6, span), jnp.float32)], axis=0)


def second_kernel(features, b_input, c_input, cum_ref, step_ref, columns, wide_row, _, out):
    intra_groups(2, features, b_input, c_input, cum_ref, step_ref, columns, wide_row, out)


def parts_of(piece):
    halves = 2
    size = (piece.shape[0] - EXTRA) // halves
    extra = piece[halves * size :, :]
    return (
        [piece[k * size : (k + 1) * size, :] for k in range(halves)],
        [extra[k : k + 1] for k in range(halves)],
        extra[halves : halves + 1],
        extra[halves + 1 : halves + 2],
    )


def write_piece(out, states, decays, keeps, amount):
    size = states[0].shape[0]
    for k, state in enumerate(states):
        out[k * size : (k + 1) * size, :] = state
    row = iota((EXTRA, LANES), 0)
    extra = jnp.where(row == len(states), keeps, amount)
    for k, decay in enumerate(decays):
        extra = jnp.where(row == k, decay, extra)
    out[len(states) * size :, :] = extra


def carry_on(states, piece):
    return [jnp.exp(decay) * old + new for old, new, decay in zip(states, piece[0], piece[1])]


def add(first, second):
    return [one + other for one, other in zip(first, second)]


def total_kernel(*refs):
    pieces, out = refs[:GROUP], refs[-1]

    @functools.partial(each_place, FIRST_ORDERS)
    def _(me, first, last):
        members = [parts_of(pieces[slot]) for slot in first]
        states, decays, keeps, _ = members[0]
        for member in members[1:]:
            states = carry_on(states, member)
            decays = add(decays, member[1])
            keeps = keeps * member[2]
        amount = members[-1][3]
        for member in members[-2::-1]:
            amount = member[3] + member[2] * amount
        write_piece(out, states, decays, keeps, amount)


def round_kernel(bit, *refs):
    total, got, before, total_out, before_out = refs
    group = lax.axis_index("ctx") // GROUP
    mine, theirs, past = parts_of(total), parts_of(got), parts_of(before)
    decays, keeps = add(mine[1], theirs[1]), mine[2] * theirs[2]

    @pl.when(lax.rem(group // bit, 2) == 1)
    def _():
        write_piece(before_out, carry_on(theirs[0], past), add(past[1], theirs[1]), past[2], past[3])
        write_piece(total_out, carry_on(theirs[0], mine), decays, keeps, theirs[3] + theirs[2] * mine[3])

    @pl.when(lax.rem(group // bit, 2) == 0)
    def _():
        write_piece(before_out, past[0], past[1], past[2] * theirs[2], past[3] + past[2] * theirs[3])
        write_piece(total_out, carry_on(mine[0], theirs), decays, keeps, mine[3] + mine[2] * theirs[3])


def entering_kernel(bit, orders, has_got, has_past, *refs):
    pieces, refs = refs[:GROUP], refs[GROUP:]
    got, refs = (refs[0], refs[1:]) if has_got else (None, refs)
    past, refs = (refs[0], refs[1:]) if has_past else (None, refs)
    outs, carry_out = refs[-GROUP - 1 : -1], refs[-1]
    is_later = lax.rem(lax.axis_index("ctx") // GROUP // bit, 2) == 1

    @functools.partial(each_place, orders)
    def _(me, first, last):
        members = [parts_of(pieces[slot]) for slot in first]
        size = members[0][0][0].shape
        arriving = [jnp.zeros(size, jnp.float32)] * 2
        keeps, amount = jnp.ones((1, LANES), jnp.float32), jnp.zeros((1, LANES), jnp.float32)
        if has_got:
            theirs = parts_of(got)
            arriving = [jnp.where(is_later, state, 0.0) for state in theirs[0]]
            keeps = jnp.where(is_later, keeps, theirs[2])
            amount = jnp.where(is_later, amount, theirs[3])
        if has_past:
            old = parts_of(past)
            arriving = carry_on(arriving, old)
            amount = old[3] + old[2] * amount
        for m in range(GROUP):
            for k, state in enumerate(arriving):
                outs[last[m]][k * size[0] : (k + 1) * size[0], :] = state
            if m < GROUP - 1:
                arriving = carry_on(arriving, members[m])
        for m in range(GROUP - 1, me, -1):
            amount = members[m][3] + members[m][2] * amount
            keeps = keeps * members[m][2]
        row = iota(carry_out.shape, 0)
        carry_out[...] = jnp.where(row == 0, amount, keeps)


def readout_kernel(orders, slots, *refs):
    entering, (c_input, columns, inside, wide_row), refs = refs[: len(slots)], refs[len(slots) :][:4], refs[len(slots) + 4 :]
    out = refs[-1]
    span, state = c_input.shape
    wide = wide_row.shape[1] // GROUP
    heads = wide_row.shape[1] // HEAD_DIM
    queries = jnp.concatenate([c_input[...]] * 2, axis=1)
    by_token = columns[:, 128:]
    squares = jnp.zeros((span, 128), jnp.float32)
    values = jnp.zeros((span, 128), jnp.float32)
    for slot, piece in zip(slots, entering):
        part = partner_index(orders, slot)
        lanes = pl.ds(pl.multiple_of(part * wide, wide), wide)
        value = jnp.concatenate([piece[:state, :], piece[state:, :]], axis=1)
        high = value.astype(jnp.bfloat16)
        low = (value - high.astype(jnp.float32)).astype(jnp.bfloat16)
        carried = dot(queries, jnp.concatenate([high, low], axis=0))
        decay = dot(by_token, selector(heads, 128, part * (heads // GROUP), wide))
        mixed = inside[:, lanes] + carried * decay
        readout = wide_row[0:1, lanes]
        squared, read = mixed * mixed, mixed * readout
        for k in range(0, wide, 128):
            squares = squares + squared[:, k : k + 128]
            values = values + read[:, k : k + 128]
    squares = jnp.sum(squares.T, axis=0, keepdims=True)
    values = jnp.sum(values.T, axis=0, keepdims=True)
    if len(refs) > 1:
        squares, values = squares + refs[0][0:1, :], values + refs[0][1:2, :]
    out[0:1, :] = squares
    out[1:2, :] = values


def last_kernel(channels, first_group_early, mine, other, suffix, carry, got, values_out, advantages_out, values, advantages, sems):
    sums = mine[...] + other[...]
    value = sums[1:2] / jnp.sqrt(sums[0:1] / channels + NORM_EPSILON)
    values[...] = value
    amount = carry[0:1, 0:1]
    if first_group_early:
        later = jnp.where(lax.axis_index("ctx") < GROUP, parts_of(got)[3][:, 0:1], 0.0)
        amount = amount + carry[1:2, 0:1] * later
    advantages[...] = suffix[0:1, :] + suffix[1:2, :] * amount - value
    copies = [
        pltpu.make_async_copy(values, values_out, sems.at[0]),
        pltpu.make_async_copy(advantages, advantages_out, sems.at[1]),
    ]
    for copy in copies:
        copy.start()
    for copy in copies:
        copy.wait()


def call(kernel, shapes, name, *args, hbm_in=False, hbm_out=False, scratch=(), aliases=None):
    near, far = pl.BlockSpec(memory_space=pltpu.VMEM), pl.BlockSpec(memory_space=pltpu.HBM)
    if hbm_in:
        args = [pltpu.with_memory_space_constraint(arg, pltpu.HBM) for arg in args]
    return pl.pallas_call(
        kernel,
        out_shape=[jax.ShapeDtypeStruct(*shape) for shape in shapes],
        in_specs=[far if hbm_in else near] * len(args),
        out_specs=[far if hbm_out else near] * len(shapes),
        scratch_shapes=scratch,
        input_output_aliases=aliases or {},
        compiler_params=pltpu.CompilerParams(vmem_limit_bytes=VMEM_BYTES),
        name=name,
    )(*args)


def swap(value, axis, mask):
    count = lax.axis_size(axis)
    return lax.ppermute(value, axis, [(k, k ^ mask) for k in range(count)])


def swap_slots(orders, pieces):
    cores = lax.axis_size("head")
    assert cores == len(orders)
    pairs = [
        [
            (k * cores + core, (k ^ orders[core][slot]) * cores + core)
            for k in range(lax.axis_size("ctx"))
            for core in range(cores)
        ]
        for slot in range(1, GROUP)
    ]
    return [lax.ppermute(piece, ("ctx", "head"), pair) for piece, pair in zip(pieces, pairs)]


def local(
    features,
    b_input,
    c_input,
    step_input,
    decay_log,
    skip_gain,
    norm_gain,
    value_weight,
    rewards,
    reward_keep_mask,
    episode_end,
):
    span, width = features.shape
    heads = step_input.shape[0]
    state = b_input.shape[1]
    halves = width // GROUP // LANES
    count = lax.axis_size("ctx")
    groups = count // GROUP
    assert span == SPAN and count == groups * GROUP and groups > 1 and groups & (groups - 1) == 0 and halves == 2
    f32, bf16, i32 = jnp.float32, jnp.bfloat16, jnp.int32
    piece = ((halves * state + EXTRA, LANES), f32)
    states = ((halves * state, LANES), f32)
    columns_shape, wide_shape, inside_shape = ((span, 256), bf16), ((2, width), f32), ((span, width), f32)

    made = call(
        state_kernel,
        [piece] * (GROUP - 1)
        + [
            ((span, width), bf16),
            ((span, state), bf16),
            ((span, state), bf16),
            ((heads, span), f32),
            ((heads, span), f32),
            ((8, span), f32),
            ((1, heads), f32),
            ((1, width), f32),
            ((1, width), f32),
            ((span, 128), f32),
            columns_shape,
            wide_shape,
            inside_shape,
        ],
        "block_states",
        step_input,
        decay_log[None, :],
        rewards[None, :],
        reward_keep_mask[None, :],
        episode_end[None, :],
        features,
        b_input,
        c_input,
        skip_gain[None, :],
        norm_gain[None, :],
        value_weight[None, :],
        hbm_in=True,
        scratch=[
            pltpu.VMEM((heads, span), f32),
            pltpu.VMEM((1, heads), f32),
            pltpu.VMEM((1, span), f32),
            pltpu.VMEM((1, span), i32),
            pltpu.VMEM((1, span), i32),
            pltpu.SemaphoreType.DMA((11,)),
        ],
    )
    pieces, made = made[: GROUP - 1], made[GROUP - 1 :]
    moved = swap_slots(FIRST_ORDERS, pieces)
    columns, wide_row, inside, suffix, own_piece = call(
        first_kernel,
        [columns_shape, wide_shape, inside_shape, ((8, span), f32), piece],
        "inside_first",
        *made,
        aliases={10: 0, 11: 1, 12: 2},
    )
    got = [own_piece, *moved]
    near = (*made[:5], columns, wide_row)
    queries = made[2]
    (total,) = call(total_kernel, [piece], "group_total", *got, suffix)
    past = None
    bit = 1
    while bit * 2 < groups:
        other = swap(total, "ctx", GROUP * bit)
        if past is None:
            row = jnp.arange(piece[0][0])[:, None]
            past = jnp.where(row == halves * (state + 1), 1.0, 0.0).astype(f32) * jnp.ones((1, LANES), f32)
        total, past = call(
            functools.partial(round_kernel, bit), [piece, piece], "scan_round", total, other, past
        )
        bit *= 2
    other = swap(total, "ctx", GROUP * bit)
    (inside,) = call(second_kernel, [inside_shape], "inside_second", *near, inside, aliases={len(near): 0})

    def finish(has_got):
        orders = LAST_ORDERS if has_got else EARLY_ORDERS
        operands = (*got, *([other] if has_got else []), *([] if past is None else [past]))
        made = call(
            functools.partial(entering_kernel, bit, orders, has_got, past is not None),
            [states] * GROUP + [((8, LANES), f32)],
            "entering_states",
            *operands,
            *([] if past is None else [inside]),
        )
        arrived = [made[0], *swap_slots(orders, made[1:GROUP])]
        sums = ()
        for slots in READOUTS:
            sums = call(
                functools.partial(readout_kernel, orders, slots),
                [((2, span), f32)],
                "readout",
                *(arrived[slot] for slot in slots),
                queries,
                columns,
                inside,
                wide_row,
                *sums,
            )
        return sums[0], made[GROUP]

    first_group_early = groups == 2
    if first_group_early:
        is_first = lax.axis_index("ctx") < GROUP
        nothing = lambda: (jnp.zeros((2, span), f32), jnp.zeros((8, LANES), f32))
        early = lax.cond(is_first, lambda: finish(False), nothing)
        sums, carry = lax.cond(is_first, lambda: early, lambda: finish(True))
    else:
        sums, carry = finish(True)
    values, advantages = call(
        functools.partial(last_kernel, width * lax.axis_size("head"), first_group_early),
        [((1, span), f32)] * 2,
        "values_and_advantages",
        sums,
        swap(sums, "head", 1),
        suffix,
        carry,
        other,
        hbm_out=True,
        scratch=[pltpu.VMEM((1, span), f32), pltpu.VMEM((1, span), f32), pltpu.SemaphoreType.DMA((2,))],
    )
    return (values[0], advantages[0])


def solution(mesh):
    placed = (
        P(("traj", "ctx"), "head"),
        P(("traj", "ctx"), None),
        P(("traj", "ctx"), None),
        P("head", ("traj", "ctx")),
        P("head"),
        P("head"),
        P("head"),
        P("head"),
        P(("traj", "ctx")),
        P(("traj", "ctx")),
        P(("traj", "ctx")),
    )
    return jax.shard_map(
        local,
        mesh=mesh,
        in_specs=placed,
        out_specs=(P(("traj", "ctx")), P(("traj", "ctx"))),
        check_vma=False,
    )
```

```python
import functools

import jax
import jax.numpy as jnp
from jax import lax
from jax.experimental import pallas as pl
from jax.experimental.pallas import tpu as pltpu
from jax.sharding import PartitionSpec as P

HEAD_DIM = 32
SPAN = 256
GROUP = 4
LANES = 128
FIRST_ORDERS = ((0, 1, 2, 3), (0, 2, 1, 3))
EARLY_ORDERS = ((0, 3, 1, 2), (0, 1, 2, 3))
LAST_ORDERS = ((0, 3, 1, 2), (0, 1, 2, 3))
READOUTS = ((0, 1, 2, 3),)
SHARES = (((0, 1, 4, 8), (0, 0, 7, 8)), ((0, 1, 6, 8), (0, 0, 6, 8)))
EXTRA = 8
NORM_EPSILON = 1e-05
VMEM_BYTES = 24 * 1024 * 1024


def split3(value):
    high = value.astype(jnp.bfloat16).astype(jnp.float32)
    rest = value - high
    middle = rest.astype(jnp.bfloat16).astype(jnp.float32)
    return high, middle, (rest - middle).astype(jnp.bfloat16).astype(jnp.float32)


def dot(a, b, contract=((1,), (0,))):
    return lax.dot_general(a, b, (contract, ((), ())), preferred_element_type=jnp.float32)


def iota(shape, dim):
    return lax.broadcasted_iota(jnp.int32, shape, dim)


def column(row):
    n = row.shape[1]
    return jnp.sum(jnp.where(iota((n, n), 0) == iota((n, n), 1), row, 0.0), axis=1, keepdims=True)


def over_channels(per_head, first_head, channels):
    heads = per_head.shape[0]
    match = iota((heads, channels), 0) == first_head + iota((heads, channels), 1) // HEAD_DIM
    return jnp.sum(jnp.where(match, per_head, 0.0), axis=0, keepdims=True)


def selector(heads, rows, first_head, channels):
    row = iota((rows, channels), 0)
    match = (lax.rem(row, heads) == first_head + iota((rows, channels), 1) // HEAD_DIM) & (row < 3 * heads)
    return jnp.where(match, 1.0, 0.0).astype(jnp.bfloat16)


def member_index():
    return lax.rem(lax.axis_index("ctx"), GROUP)


def partner_index(orders, slot):
    return lax.bitwise_xor(member_index(), jnp.where(lax.axis_index("head") == 0, orders[0][slot], orders[1][slot]))


def each_place(last_orders, body):
    for core in range(len(FIRST_ORDERS)):
        for v in range(GROUP):

            @pl.when((member_index() == v) & (lax.axis_index("head") == core))
            def _():
                body(v, *([orders[core].index(v ^ m) for m in range(GROUP)] for orders in (FIRST_ORDERS, last_orders)))


def prepare(cum_ref, skip, norm, weight, columns_out, wide_out):
    heads, span = cum_ref.shape
    cum = cum_ref[...]
    pad = jnp.zeros((128 - 3 * heads, span), jnp.float32)
    columns_out[:, :128] = jnp.concatenate(split3(cum) + (jnp.ones_like(pad),), axis=0).T.astype(jnp.bfloat16)
    columns_out[:, 128:] = jnp.concatenate(split3(jnp.exp(cum)) + (pad,), axis=0).T.astype(jnp.bfloat16)
    wide_out[0:1, :] = norm[...] * weight[...]
    wide_out[1:2, :] = over_channels(column(skip[...]), 0, heads * HEAD_DIM)


def write_pieces(slots, token, features, b_input, total, still_open, first_sum, outs):
    keys = b_input[...].T
    state = keys.shape[0]
    heads = total.shape[0]
    wide = features.shape[1] // GROUP
    row = iota((EXTRA, LANES), 0)
    by_token = token[...].astype(jnp.bfloat16)
    for slot, out in zip(slots, outs):
        part = partner_index(FIRST_ORDERS, slot)
        first_head = part * (heads // GROUP)
        feat = features[:, pl.ds(pl.multiple_of(part * wide, wide), wide)]
        spread = dot(by_token, selector(heads, 128, first_head, wide))
        scaled = (spread * feat.astype(jnp.float32)).astype(jnp.bfloat16)
        states = dot(keys, scaled)
        decay = over_channels(total, first_head, wide)
        extra = jnp.where(row == wide // LANES, still_open, first_sum)
        for k in range(wide // LANES):
            out[k * state : (k + 1) * state, :] = states[:, k * LANES : (k + 1) * LANES]
            extra = jnp.where(row == k, decay[:, k * LANES : (k + 1) * LANES], extra)
        out[wide // LANES * state :, :] = extra


def state_kernel(*refs):
    sources, refs = refs[:11], refs[11:]
    pieces, refs = refs[: GROUP - 1], refs[GROUP - 1 :]
    features, b_input, c_input, cum_out, step_out, rows, skip, norm, weight, token, columns, wide_row, inside = refs[:13]
    step_in, decay_log, rewards, keep, ends, sems = refs[13:]
    targets = (step_in, decay_log, rewards, keep, ends, features, b_input, c_input, skip, norm, weight)
    copies = [pltpu.make_async_copy(src, dst, sems.at[i]) for i, (src, dst) in enumerate(zip(sources, targets))]
    for copy in copies:
        copy.start()
    heads, span = step_in.shape
    for copy in copies[:5]:
        copy.wait()
    raw = step_in[...]
    step = jnp.maximum(raw, 0.0) + jnp.log1p(jnp.exp(-jnp.abs(raw)))
    log_decay = -jnp.exp(column(decay_log[...])) * step
    ends_row = ends[...].astype(jnp.float32)
    live = keep[...].astype(jnp.float32) * rewards[...]
    upper = jnp.where(iota((span, span), 0) <= iota((span, span), 1), 1.0, 0.0).astype(jnp.bfloat16)
    stacked = jnp.concatenate(split3(log_decay) + (jnp.broadcast_to(ends_row, (16, span)),), axis=0)
    summed = dot(stacked.astype(jnp.bfloat16), upper)
    cum = summed[:heads] + summed[heads : 2 * heads] + summed[2 * heads : 3 * heads]
    through = summed[3 * heads : 3 * heads + 1]
    before = through - ends_row
    total = cum[:, span - 1 :]
    first_sum = jnp.sum(jnp.where(before == 0.0, live, 0.0), axis=1, keepdims=True)
    still_open = jnp.where(through[:, span - 1 :] == 0.0, 1.0, 0.0)
    coefficient = jnp.exp(total - cum) * step
    pad = jnp.zeros((128 - 3 * heads, span), jnp.float32)
    token[...] = jnp.concatenate(split3(coefficient) + (pad,), axis=0).T
    cum_out[...] = cum
    step_out[...] = step
    flags = [jnp.broadcast_to(value, (1, span)) for value in (still_open, first_sum)]
    rows[...] = jnp.concatenate([live, through, before, *flags, jnp.zeros((3, span), jnp.float32)], axis=0)
    for copy in copies[5:]:
        copy.wait()

    @pl.when(share_bound(1) > 0)
    def _():
        prepare(cum_out, skip, norm, weight, columns, wide_row)
        intra_groups(0, features, b_input, c_input, cum_out, step_out, columns, wide_row, inside)

    write_pieces((1, 2, 3), token, features, b_input, total, still_open, first_sum, pieces)


def share_bound(k):
    first_group, first_core = lax.axis_index("ctx") < GROUP, lax.axis_index("head") == 0
    return jnp.where(
        first_group,
        jnp.where(first_core, SHARES[0][0][k], SHARES[0][1][k]),
        jnp.where(first_core, SHARES[1][0][k], SHARES[1][1][k]),
    )


def intra_groups(stage, features, b_input, c_input, cum_ref, step_ref, columns, wide_row, out):
    start, stop = share_bound(stage), share_bound(stage + 1)
    heads, span = cum_ref.shape
    at_once = 128 // HEAD_DIM
    t, s = iota((span, span), 0), iota((span, span), 1)
    scores = jnp.where(t >= s, dot(c_input[...], b_input[...], ((1,), (1,))), 0.0)
    by_token = columns[:, :128]
    row = iota((128, span), 0)

    def some_heads(index, carry):
        first = index * at_once
        lanes = pl.ds(pl.multiple_of(index * 128, 128), 128)
        feat = features[:, lanes]
        total = feat.astype(jnp.float32) * wide_row[1:2, lanes]
        owner = iota((span, 128), 1) // HEAD_DIM
        for j in range(at_once):
            head = first + j
            cum = cum_ref[pl.ds(head, 1), :]
            high, middle, low = split3(cum)
            other = jnp.where(
                row < 3 * heads,
                jnp.where(lax.rem(row, heads) == head, 1.0, 0.0),
                jnp.where(
                    row == 3 * heads,
                    -high,
                    jnp.where(row == 3 * heads + 1, -middle, jnp.where(row == 3 * heads + 2, -low, 0.0)),
                ),
            ).astype(jnp.bfloat16)
            gap = jnp.minimum(dot(by_token, other), 0.0)
            weights = (scores * jnp.exp(gap) * step_ref[pl.ds(head, 1), :]).astype(jnp.bfloat16)
            total = total + dot(weights, jnp.where(owner == j, feat, jnp.zeros_like(feat)))
        out[:, lanes] = total
        return carry

    lax.fori_loop(start, stop, some_heads, 0)


def first_kernel(
    features,
    b_input,
    c_input,
    cum_ref,
    step_ref,
    rows,
    skip,
    norm,
    weight,
    token,
    _0,
    _1,
    _2,
    columns,
    wide_row,
    out,
    suffix,
    own_piece,
):
    span = cum_ref.shape[1]
    write_pieces(
        (0,), token, features, b_input, cum_ref[:, span - 1 :], rows[3:4, 0:1], rows[4:5, 0:1], (own_piece,)
    )

    @pl.when(share_bound(1) == 0)
    def _():
        prepare(cum_ref, skip, norm, weight, columns, wide_row)

    intra_groups(1, features, b_input, c_input, cum_ref, step_ref, columns, wide_row, out)

    t, s = iota((span, span), 0), iota((span, span), 1)
    live, through, before = rows[0:1, :], rows[1:2, :], rows[2:3, :]
    reach = jnp.where((t >= s) & (column(before) == before), column(live), 0.0)
    sums = jnp.sum(reach, axis=0, keepdims=True)
    open_end = jnp.where(before == through[:, span - 1 :], 1.0, 0.0)
    suffix[...] = jnp.concatenate([sums, open_end, jnp.zeros((6, span), jnp.float32)], axis=0)


def second_kernel(features, b_input, c_input, cum_ref, step_ref, columns, wide_row, _, out):
    intra_groups(2, features, b_input, c_input, cum_ref, step_ref, columns, wide_row, out)


def parts_of(piece):
    halves = 2
    size = (piece.shape[0] - EXTRA) // halves
    extra = piece[halves * size :, :]
    return (
        [piece[k * size : (k + 1) * size, :] for k in range(halves)],
        [extra[k : k + 1] for k in range(halves)],
        extra[halves : halves + 1],
        extra[halves + 1 : halves + 2],
    )


def write_piece(out, states, decays, keeps, amount):
    size = states[0].shape[0]
    for k, state in enumerate(states):
        out[k * size : (k + 1) * size, :] = state
    row = iota((EXTRA, LANES), 0)
    extra = jnp.where(row == len(states), keeps, amount)
    for k, decay in enumerate(decays):
        extra = jnp.where(row == k, decay, extra)
    out[len(states) * size :, :] = extra


def carry_on(states, piece):
    return [jnp.exp(decay) * old + new for old, new, decay in zip(states, piece[0], piece[1])]


def add(first, second):
    return [one + other for one, other in zip(first, second)]


def total_kernel(two_groups, *refs):
    pieces, out = refs[:GROUP], refs[-1]

    @functools.partial(each_place, FIRST_ORDERS)
    def _(me, first, last):
        members = [parts_of(pieces[slot]) for slot in first]
        states, decays, keeps, _ = members[0]
        for member in members[1:]:
            states = carry_on(states, member)
            decays = add(decays, member[1])
            keeps = keeps * member[2]
        amount = members[-1][3]
        for member in members[-2::-1]:
            amount = member[3] + member[2] * amount
        if not two_groups:
            write_piece(out, states, decays, keeps, amount)
            return

        @pl.when(lax.axis_index("ctx") < GROUP)
        def _():
            for k, state in enumerate(states):
                out[k * state.shape[0] : (k + 1) * state.shape[0], :] = state

        @pl.when(lax.axis_index("ctx") >= GROUP)
        def _():
            out[:EXTRA, :] = jnp.broadcast_to(amount, (EXTRA, LANES))


def round_kernel(bit, *refs):
    total, got, before, total_out, before_out = refs
    group = lax.axis_index("ctx") // GROUP
    mine, theirs, past = parts_of(total), parts_of(got), parts_of(before)
    decays, keeps = add(mine[1], theirs[1]), mine[2] * theirs[2]

    @pl.when(lax.rem(group // bit, 2) == 1)
    def _():
        write_piece(before_out, carry_on(theirs[0], past), add(past[1], theirs[1]), past[2], past[3])
        write_piece(total_out, carry_on(theirs[0], mine), decays, keeps, theirs[3] + theirs[2] * mine[3])

    @pl.when(lax.rem(group // bit, 2) == 0)
    def _():
        write_piece(before_out, past[0], past[1], past[2] * theirs[2], past[3] + past[2] * theirs[3])
        write_piece(total_out, carry_on(mine[0], theirs), decays, keeps, mine[3] + mine[2] * theirs[3])


def entering_kernel(bit, orders, has_got, has_past, *refs):
    pieces, refs = refs[:GROUP], refs[GROUP:]
    got, refs = (refs[0], refs[1:]) if has_got else (None, refs)
    past, refs = (refs[0], refs[1:]) if has_past else (None, refs)
    outs, carry_out = refs[-GROUP - 1 : -1], refs[-1]
    is_later = lax.rem(lax.axis_index("ctx") // GROUP // bit, 2) == 1

    @functools.partial(each_place, orders)
    def _(me, first, last):
        members = [parts_of(pieces[slot]) for slot in first]
        size = members[0][0][0].shape
        arriving = [jnp.zeros(size, jnp.float32)] * 2
        keeps, amount = jnp.ones((1, LANES), jnp.float32), jnp.zeros((1, LANES), jnp.float32)
        if has_got and got.shape[0] == 2 * size[0]:
            arriving = [got[: size[0], :], got[size[0] :, :]]
        elif has_got:
            theirs = parts_of(got)
            arriving = [jnp.where(is_later, state, 0.0) for state in theirs[0]]
            keeps = jnp.where(is_later, keeps, theirs[2])
            amount = jnp.where(is_later, amount, theirs[3])
        if has_past:
            old = parts_of(past)
            arriving = carry_on(arriving, old)
            amount = old[3] + old[2] * amount
        for m in range(GROUP):
            for k, state in enumerate(arriving):
                outs[last[m]][k * size[0] : (k + 1) * size[0], :] = state
            if m < GROUP - 1:
                arriving = carry_on(arriving, members[m])
        for m in range(GROUP - 1, me, -1):
            amount = members[m][3] + members[m][2] * amount
            keeps = keeps * members[m][2]
        row = iota(carry_out.shape, 0)
        carry_out[...] = jnp.where(row == 0, amount, keeps)


def readout_kernel(orders, slots, *refs):
    entering, (c_input, columns, inside, wide_row), refs = refs[: len(slots)], refs[len(slots) :][:4], refs[len(slots) + 4 :]
    out = refs[-1]
    span, state = c_input.shape
    wide = wide_row.shape[1] // GROUP
    heads = wide_row.shape[1] // HEAD_DIM
    queries = jnp.concatenate([c_input[...]] * 2, axis=1)
    by_token = columns[:, 128:]
    squares = jnp.zeros((span, 128), jnp.float32)
    values = jnp.zeros((span, 128), jnp.float32)
    for slot, piece in zip(slots, entering):
        part = partner_index(orders, slot)
        lanes = pl.ds(pl.multiple_of(part * wide, wide), wide)
        value = jnp.concatenate([piece[:state, :], piece[state:, :]], axis=1)
        high = value.astype(jnp.bfloat16)
        low = (value - high.astype(jnp.float32)).astype(jnp.bfloat16)
        carried = dot(queries, jnp.concatenate([high, low], axis=0))
        decay = dot(by_token, selector(heads, 128, part * (heads // GROUP), wide))
        mixed = inside[:, lanes] + carried * decay
        readout = wide_row[0:1, lanes]
        squared, read = mixed * mixed, mixed * readout
        for k in range(0, wide, 128):
            squares = squares + squared[:, k : k + 128]
            values = values + read[:, k : k + 128]
    squares = jnp.sum(squares.T, axis=0, keepdims=True)
    values = jnp.sum(values.T, axis=0, keepdims=True)
    if len(refs) > 1:
        squares, values = squares + refs[0][0:1, :], values + refs[0][1:2, :]
    out[0:1, :] = squares
    out[1:2, :] = values


def last_kernel(channels, first_group_early, mine, other, suffix, carry, got, values_out, advantages_out, values, advantages, sems):
    sums = mine[...] + other[...]
    value = sums[1:2] / jnp.sqrt(sums[0:1] / channels + NORM_EPSILON)
    values[...] = value
    amount = carry[0:1, 0:1]
    if first_group_early:
        later = jnp.where(lax.axis_index("ctx") < GROUP, got[0:1, 0:1], 0.0)
        amount = amount + carry[1:2, 0:1] * later
    advantages[...] = suffix[0:1, :] + suffix[1:2, :] * amount - value
    copies = [
        pltpu.make_async_copy(values, values_out, sems.at[0]),
        pltpu.make_async_copy(advantages, advantages_out, sems.at[1]),
    ]
    for copy in copies:
        copy.start()
    for copy in copies:
        copy.wait()


def call(kernel, shapes, name, *args, hbm_in=False, hbm_out=False, scratch=(), aliases=None):
    near, far = pl.BlockSpec(memory_space=pltpu.VMEM), pl.BlockSpec(memory_space=pltpu.HBM)
    if hbm_in:
        args = [pltpu.with_memory_space_constraint(arg, pltpu.HBM) for arg in args]
    return pl.pallas_call(
        kernel,
        out_shape=[jax.ShapeDtypeStruct(*shape) for shape in shapes],
        in_specs=[far if hbm_in else near] * len(args),
        out_specs=[far if hbm_out else near] * len(shapes),
        scratch_shapes=scratch,
        input_output_aliases=aliases or {},
        compiler_params=pltpu.CompilerParams(vmem_limit_bytes=VMEM_BYTES),
        name=name,
    )(*args)


def swap(value, axis, mask):
    count = lax.axis_size(axis)
    return lax.ppermute(value, axis, [(k, k ^ mask) for k in range(count)])


def swap_slots(orders, pieces):
    cores = lax.axis_size("head")
    assert cores == len(orders)
    pairs = [
        [
            (k * cores + core, (k ^ orders[core][slot]) * cores + core)
            for k in range(lax.axis_size("ctx"))
            for core in range(cores)
        ]
        for slot in range(1, GROUP)
    ]
    return [lax.ppermute(piece, ("ctx", "head"), pair) for piece, pair in zip(pieces, pairs)]


def local(
    features,
    b_input,
    c_input,
    step_input,
    decay_log,
    skip_gain,
    norm_gain,
    value_weight,
    rewards,
    reward_keep_mask,
    episode_end,
):
    span, width = features.shape
    heads = step_input.shape[0]
    state = b_input.shape[1]
    halves = width // GROUP // LANES
    count = lax.axis_size("ctx")
    groups = count // GROUP
    assert span == SPAN and count == groups * GROUP and groups > 1 and groups & (groups - 1) == 0 and halves == 2
    f32, bf16, i32 = jnp.float32, jnp.bfloat16, jnp.int32
    piece = ((halves * state + EXTRA, LANES), f32)
    states = ((halves * state, LANES), f32)
    columns_shape, wide_shape, inside_shape = ((span, 256), bf16), ((2, width), f32), ((span, width), f32)

    made = call(
        state_kernel,
        [piece] * (GROUP - 1)
        + [
            ((span, width), bf16),
            ((span, state), bf16),
            ((span, state), bf16),
            ((heads, span), f32),
            ((heads, span), f32),
            ((8, span), f32),
            ((1, heads), f32),
            ((1, width), f32),
            ((1, width), f32),
            ((span, 128), f32),
            columns_shape,
            wide_shape,
            inside_shape,
        ],
        "block_states",
        step_input,
        decay_log[None, :],
        rewards[None, :],
        reward_keep_mask[None, :],
        episode_end[None, :],
        features,
        b_input,
        c_input,
        skip_gain[None, :],
        norm_gain[None, :],
        value_weight[None, :],
        hbm_in=True,
        scratch=[
            pltpu.VMEM((heads, span), f32),
            pltpu.VMEM((1, heads), f32),
            pltpu.VMEM((1, span), f32),
            pltpu.VMEM((1, span), i32),
            pltpu.VMEM((1, span), i32),
            pltpu.SemaphoreType.DMA((11,)),
        ],
    )
    pieces, made = made[: GROUP - 1], made[GROUP - 1 :]
    moved = swap_slots(FIRST_ORDERS, pieces)
    columns, wide_row, inside, suffix, own_piece = call(
        first_kernel,
        [columns_shape, wide_shape, inside_shape, ((8, span), f32), piece],
        "inside_first",
        *made,
        aliases={10: 0, 11: 1, 12: 2},
    )
    got = [own_piece, *moved]
    near = (*made[:5], columns, wide_row)
    queries = made[2]
    (total,) = call(
        functools.partial(total_kernel, groups == 2),
        [states if groups == 2 else piece],
        "group_total",
        *got,
        suffix,
    )
    past = None
    bit = 1
    while bit * 2 < groups:
        other = swap(total, "ctx", GROUP * bit)
        if past is None:
            row = jnp.arange(piece[0][0])[:, None]
            past = jnp.where(row == halves * (state + 1), 1.0, 0.0).astype(f32) * jnp.ones((1, LANES), f32)
        total, past = call(
            functools.partial(round_kernel, bit), [piece, piece], "scan_round", total, other, past
        )
        bit *= 2
    other = swap(total, "ctx", GROUP * bit)
    (inside,) = call(second_kernel, [inside_shape], "inside_second", *near, inside, aliases={len(near): 0})

    def finish(has_got):
        orders = LAST_ORDERS if has_got else EARLY_ORDERS
        operands = (*got, *([other] if has_got else []), *([] if past is None else [past]))
        made = call(
            functools.partial(entering_kernel, bit, orders, has_got, past is not None),
            [states] * GROUP + [((8, LANES), f32)],
            "entering_states",
            *operands,
            *([] if past is None else [inside]),
        )
        arrived = [made[0], *swap_slots(orders, made[1:GROUP])]
        sums = ()
        for slots in READOUTS:
            sums = call(
                functools.partial(readout_kernel, orders, slots),
                [((2, span), f32)],
                "readout",
                *(arrived[slot] for slot in slots),
                queries,
                columns,
                inside,
                wide_row,
                *sums,
            )
        return sums[0], made[GROUP]

    first_group_early = groups == 2
    if first_group_early:
        is_first = lax.axis_index("ctx") < GROUP
        nothing = lambda: (jnp.zeros((2, span), f32), jnp.zeros((8, LANES), f32))
        early = lax.cond(is_first, lambda: finish(False), nothing)
        sums, carry = lax.cond(is_first, lambda: early, lambda: finish(True))
    else:
        sums, carry = finish(True)
    values, advantages = call(
        functools.partial(last_kernel, width * lax.axis_size("head"), first_group_early),
        [((1, span), f32)] * 2,
        "values_and_advantages",
        sums,
        swap(sums, "head", 1),
        suffix,
        carry,
        other,
        hbm_out=True,
        scratch=[pltpu.VMEM((1, span), f32), pltpu.VMEM((1, span), f32), pltpu.SemaphoreType.DMA((2,))],
    )
    return (values[0], advantages[0])


def solution(mesh):
    placed = (
        P(("traj", "ctx"), "head"),
        P(("traj", "ctx"), None),
        P(("traj", "ctx"), None),
        P("head", ("traj", "ctx")),
        P("head"),
        P("head"),
        P("head"),
        P("head"),
        P(("traj", "ctx")),
        P(("traj", "ctx")),
        P(("traj", "ctx")),
    )
    return jax.shard_map(
        local,
        mesh=mesh,
        in_specs=placed,
        out_specs=(P(("traj", "ctx")), P(("traj", "ctx"))),
        check_vma=False,
    )
```

```python
import functools

import jax
import jax.numpy as jnp
from jax import lax
from jax.experimental import pallas as pl
from jax.experimental.pallas import tpu as pltpu
from jax.sharding import PartitionSpec as P

HEAD_DIM = 32
SPAN = 256
GROUP = 4
LANES = 128
FIRST_ORDERS = ((0, 1, 2, 3), (0, 2, 1, 3))
EARLY_ORDERS = ((0, 3, 1, 2), (0, 1, 2, 3))
LAST_ORDERS = ((0, 3, 1, 2), (0, 1, 2, 3))
READOUTS = ((0, 1, 2, 3),)
SHARES = (((0, 1, 4, 8), (0, 0, 7, 8)), ((0, 1, 6, 8), (0, 0, 6, 8)))
EXTRA = 8
NORM_EPSILON = 1e-05
VMEM_BYTES = 24 * 1024 * 1024


def split3(value):
    high = value.astype(jnp.bfloat16).astype(jnp.float32)
    rest = value - high
    middle = rest.astype(jnp.bfloat16).astype(jnp.float32)
    return high, middle, (rest - middle).astype(jnp.bfloat16).astype(jnp.float32)


def dot(a, b, contract=((1,), (0,))):
    return lax.dot_general(a, b, (contract, ((), ())), preferred_element_type=jnp.float32)


def iota(shape, dim):
    return lax.broadcasted_iota(jnp.int32, shape, dim)


def column(row):
    n = row.shape[1]
    return jnp.sum(jnp.where(iota((n, n), 0) == iota((n, n), 1), row, 0.0), axis=1, keepdims=True)


def over_channels(per_head, first_head, channels):
    heads = per_head.shape[0]
    match = iota((heads, channels), 0) == first_head + iota((heads, channels), 1) // HEAD_DIM
    return jnp.sum(jnp.where(match, per_head, 0.0), axis=0, keepdims=True)


def selector(heads, rows, first_head, channels):
    row = iota((rows, channels), 0)
    match = (lax.rem(row, heads) == first_head + iota((rows, channels), 1) // HEAD_DIM) & (row < 3 * heads)
    return jnp.where(match, 1.0, 0.0).astype(jnp.bfloat16)


def member_index():
    return lax.rem(lax.axis_index("ctx"), GROUP)


def partner_index(orders, slot):
    return lax.bitwise_xor(member_index(), jnp.where(lax.axis_index("head") == 0, orders[0][slot], orders[1][slot]))


def each_place(last_orders, body):
    for core in range(len(FIRST_ORDERS)):
        for v in range(GROUP):

            @pl.when((member_index() == v) & (lax.axis_index("head") == core))
            def _():
                body(v, *([orders[core].index(v ^ m) for m in range(GROUP)] for orders in (FIRST_ORDERS, last_orders)))


def prepare(cum_ref, skip, norm, weight, columns_out, wide_out):
    heads, span = cum_ref.shape
    cum = cum_ref[...]
    pad = jnp.zeros((128 - 3 * heads, span), jnp.float32)
    columns_out[:, :128] = jnp.concatenate(split3(cum) + (jnp.ones_like(pad),), axis=0).T.astype(jnp.bfloat16)
    columns_out[:, 128:] = jnp.concatenate(split3(jnp.exp(cum)) + (pad,), axis=0).T.astype(jnp.bfloat16)
    wide_out[0:1, :] = norm[...] * weight[...]
    wide_out[1:2, :] = over_channels(column(skip[...]), 0, heads * HEAD_DIM)


def write_pieces(slots, token, features, b_input, total, still_open, first_sum, outs):
    keys = b_input[...].T
    state = keys.shape[0]
    heads = total.shape[0]
    wide = features.shape[1] // GROUP
    row = iota((EXTRA, LANES), 0)
    by_token = token[...].astype(jnp.bfloat16)
    places = [partner_index(FIRST_ORDERS, slot) for slot in slots]
    spread = [dot(by_token, selector(heads, 128, part * (heads // GROUP), wide)) for part in places]
    feats = [features[:, pl.ds(pl.multiple_of(part * wide, wide), wide)] for part in places]
    scaled = [(one * feat.astype(jnp.float32)).astype(jnp.bfloat16) for one, feat in zip(spread, feats)]
    states = [dot(keys, one) for one in scaled]
    for part, one, out in zip(places, states, outs):
        decay = over_channels(total, part * (heads // GROUP), wide)
        extra = jnp.where(row == wide // LANES, still_open, first_sum)
        for k in range(wide // LANES):
            out[k * state : (k + 1) * state, :] = one[:, k * LANES : (k + 1) * LANES]
            extra = jnp.where(row == k, decay[:, k * LANES : (k + 1) * LANES], extra)
        out[wide // LANES * state :, :] = extra


def state_kernel(*refs):
    sources, refs = refs[:11], refs[11:]
    pieces, refs = refs[: GROUP - 1], refs[GROUP - 1 :]
    features, b_input, c_input, cum_out, step_out, rows, skip, norm, weight, token, columns, wide_row, inside = refs[:13]
    step_in, decay_log, rewards, keep, ends, sems = refs[13:]
    targets = (step_in, decay_log, rewards, keep, ends, features, b_input, c_input, skip, norm, weight)
    copies = [pltpu.make_async_copy(src, dst, sems.at[i]) for i, (src, dst) in enumerate(zip(sources, targets))]
    for copy in copies:
        copy.start()
    heads, span = step_in.shape
    for copy in copies[:5]:
        copy.wait()
    raw = step_in[...]
    step = jnp.maximum(raw, 0.0) + jnp.log1p(jnp.exp(-jnp.abs(raw)))
    log_decay = -jnp.exp(column(decay_log[...])) * step
    ends_row = ends[...].astype(jnp.float32)
    live = keep[...].astype(jnp.float32) * rewards[...]
    upper = jnp.where(iota((span, span), 0) <= iota((span, span), 1), 1.0, 0.0).astype(jnp.bfloat16)
    stacked = jnp.concatenate(split3(log_decay) + (jnp.broadcast_to(ends_row, (16, span)),), axis=0)
    summed = dot(stacked.astype(jnp.bfloat16), upper)
    cum = summed[:heads] + summed[heads : 2 * heads] + summed[2 * heads : 3 * heads]
    through = summed[3 * heads : 3 * heads + 1]
    before = through - ends_row
    total = cum[:, span - 1 :]
    first_sum = jnp.sum(jnp.where(before == 0.0, live, 0.0), axis=1, keepdims=True)
    still_open = jnp.where(through[:, span - 1 :] == 0.0, 1.0, 0.0)
    coefficient = jnp.exp(total - cum) * step
    pad = jnp.zeros((128 - 3 * heads, span), jnp.float32)
    token[...] = jnp.concatenate(split3(coefficient) + (pad,), axis=0).T
    cum_out[...] = cum
    step_out[...] = step
    flags = [jnp.broadcast_to(value, (1, span)) for value in (still_open, first_sum)]
    rows[...] = jnp.concatenate([live, through, before, *flags, jnp.zeros((3, span), jnp.float32)], axis=0)
    for copy in copies[5:]:
        copy.wait()

    @pl.when(share_bound(1) > 0)
    def _():
        prepare(cum_out, skip, norm, weight, columns, wide_row)
        intra_groups(0, features, b_input, c_input, cum_out, step_out, columns, wide_row, inside)

    write_pieces((1, 2, 3), token, features, b_input, total, still_open, first_sum, pieces)


def share_bound(k):
    first_group, first_core = lax.axis_index("ctx") < GROUP, lax.axis_index("head") == 0
    return jnp.where(
        first_group,
        jnp.where(first_core, SHARES[0][0][k], SHARES[0][1][k]),
        jnp.where(first_core, SHARES[1][0][k], SHARES[1][1][k]),
    )


def intra_groups(stage, features, b_input, c_input, cum_ref, step_ref, columns, wide_row, out):
    start, stop = share_bound(stage), share_bound(stage + 1)
    heads, span = cum_ref.shape
    at_once = 128 // HEAD_DIM
    t, s = iota((span, span), 0), iota((span, span), 1)
    scores = jnp.where(t >= s, dot(c_input[...], b_input[...], ((1,), (1,))), 0.0)
    by_token = columns[:, :128]
    row = iota((128, span), 0)

    def some_heads(index, carry):
        first = index * at_once
        lanes = pl.ds(pl.multiple_of(index * 128, 128), 128)
        feat = features[:, lanes]
        total = feat.astype(jnp.float32) * wide_row[1:2, lanes]
        owner = iota((span, 128), 1) // HEAD_DIM
        for j in range(at_once):
            head = first + j
            cum = cum_ref[pl.ds(head, 1), :]
            high, middle, low = split3(cum)
            other = jnp.where(
                row < 3 * heads,
                jnp.where(lax.rem(row, heads) == head, 1.0, 0.0),
                jnp.where(
                    row == 3 * heads,
                    -high,
                    jnp.where(row == 3 * heads + 1, -middle, jnp.where(row == 3 * heads + 2, -low, 0.0)),
                ),
            ).astype(jnp.bfloat16)
            gap = jnp.minimum(dot(by_token, other), 0.0)
            weights = (scores * jnp.exp(gap) * step_ref[pl.ds(head, 1), :]).astype(jnp.bfloat16)
            total = total + dot(weights, jnp.where(owner == j, feat, jnp.zeros_like(feat)))
        out[:, lanes] = total
        return carry

    lax.fori_loop(start, stop, some_heads, 0)


def first_kernel(
    features,
    b_input,
    c_input,
    cum_ref,
    step_ref,
    rows,
    skip,
    norm,
    weight,
    token,
    _0,
    _1,
    _2,
    columns,
    wide_row,
    out,
    suffix,
    own_piece,
):
    span = cum_ref.shape[1]
    write_pieces(
        (0,), token, features, b_input, cum_ref[:, span - 1 :], rows[3:4, 0:1], rows[4:5, 0:1], (own_piece,)
    )

    @pl.when(share_bound(1) == 0)
    def _():
        prepare(cum_ref, skip, norm, weight, columns, wide_row)

    intra_groups(1, features, b_input, c_input, cum_ref, step_ref, columns, wide_row, out)

    t, s = iota((span, span), 0), iota((span, span), 1)
    live, through, before = rows[0:1, :], rows[1:2, :], rows[2:3, :]
    reach = jnp.where((t >= s) & (column(before) == before), column(live), 0.0)
    sums = jnp.sum(reach, axis=0, keepdims=True)
    open_end = jnp.where(before == through[:, span - 1 :], 1.0, 0.0)
    suffix[...] = jnp.concatenate([sums, open_end, jnp.zeros((6, span), jnp.float32)], axis=0)


def second_kernel(features, b_input, c_input, cum_ref, step_ref, columns, wide_row, _, out):
    intra_groups(2, features, b_input, c_input, cum_ref, step_ref, columns, wide_row, out)


def parts_of(piece):
    halves = 2
    size = (piece.shape[0] - EXTRA) // halves
    extra = piece[halves * size :, :]
    return (
        [piece[k * size : (k + 1) * size, :] for k in range(halves)],
        [extra[k : k + 1] for k in range(halves)],
        extra[halves : halves + 1],
        extra[halves + 1 : halves + 2],
    )


def write_piece(out, states, decays, keeps, amount):
    size = states[0].shape[0]
    for k, state in enumerate(states):
        out[k * size : (k + 1) * size, :] = state
    row = iota((EXTRA, LANES), 0)
    extra = jnp.where(row == len(states), keeps, amount)
    for k, decay in enumerate(decays):
        extra = jnp.where(row == k, decay, extra)
    out[len(states) * size :, :] = extra


def carry_on(states, piece):
    return [jnp.exp(decay) * old + new for old, new, decay in zip(states, piece[0], piece[1])]


def add(first, second):
    return [one + other for one, other in zip(first, second)]


def total_kernel(two_groups, *refs):
    pieces, out = refs[:GROUP], refs[-1]

    @functools.partial(each_place, FIRST_ORDERS)
    def _(me, first, last):
        members = [parts_of(pieces[slot]) for slot in first]
        states, decays, keeps, _ = members[0]
        for member in members[1:]:
            states = carry_on(states, member)
            decays = add(decays, member[1])
            keeps = keeps * member[2]
        amount = members[-1][3]
        for member in members[-2::-1]:
            amount = member[3] + member[2] * amount
        if not two_groups:
            write_piece(out, states, decays, keeps, amount)
            return

        @pl.when(lax.axis_index("ctx") < GROUP)
        def _():
            for k, state in enumerate(states):
                out[k * state.shape[0] : (k + 1) * state.shape[0], :] = state

        @pl.when(lax.axis_index("ctx") >= GROUP)
        def _():
            out[:EXTRA, :] = jnp.broadcast_to(amount, (EXTRA, LANES))


def round_kernel(bit, *refs):
    total, got, before, total_out, before_out = refs
    group = lax.axis_index("ctx") // GROUP
    mine, theirs, past = parts_of(total), parts_of(got), parts_of(before)
    decays, keeps = add(mine[1], theirs[1]), mine[2] * theirs[2]

    @pl.when(lax.rem(group // bit, 2) == 1)
    def _():
        write_piece(before_out, carry_on(theirs[0], past), add(past[1], theirs[1]), past[2], past[3])
        write_piece(total_out, carry_on(theirs[0], mine), decays, keeps, theirs[3] + theirs[2] * mine[3])

    @pl.when(lax.rem(group // bit, 2) == 0)
    def _():
        write_piece(before_out, past[0], past[1], past[2] * theirs[2], past[3] + past[2] * theirs[3])
        write_piece(total_out, carry_on(mine[0], theirs), decays, keeps, mine[3] + mine[2] * theirs[3])


def entering_kernel(bit, orders, has_got, has_past, *refs):
    pieces, refs = refs[:GROUP], refs[GROUP:]
    got, refs = (refs[0], refs[1:]) if has_got else (None, refs)
    past, refs = (refs[0], refs[1:]) if has_past else (None, refs)
    outs, carry_out = refs[-GROUP - 1 : -1], refs[-1]
    is_later = lax.rem(lax.axis_index("ctx") // GROUP // bit, 2) == 1

    @functools.partial(each_place, orders)
    def _(me, first, last):
        members = [parts_of(pieces[slot]) for slot in first]
        size = members[0][0][0].shape
        arriving = [jnp.zeros(size, jnp.float32)] * 2
        keeps, amount = jnp.ones((1, LANES), jnp.float32), jnp.zeros((1, LANES), jnp.float32)
        if has_got and got.shape[0] == 2 * size[0]:
            arriving = [got[: size[0], :], got[size[0] :, :]]
        elif has_got:
            theirs = parts_of(got)
            arriving = [jnp.where(is_later, state, 0.0) for state in theirs[0]]
            keeps = jnp.where(is_later, keeps, theirs[2])
            amount = jnp.where(is_later, amount, theirs[3])
        if has_past:
            old = parts_of(past)
            arriving = carry_on(arriving, old)
            amount = old[3] + old[2] * amount
        for m in range(GROUP):
            for k, state in enumerate(arriving):
                outs[last[m]][k * size[0] : (k + 1) * size[0], :] = state
            if m < GROUP - 1:
                arriving = carry_on(arriving, members[m])
        for m in range(GROUP - 1, me, -1):
            amount = members[m][3] + members[m][2] * amount
            keeps = keeps * members[m][2]
        row = iota(carry_out.shape, 0)
        carry_out[...] = jnp.where(row == 0, amount, keeps)


def readout_kernel(orders, slots, *refs):
    entering, (c_input, columns, inside, wide_row), refs = refs[: len(slots)], refs[len(slots) :][:4], refs[len(slots) + 4 :]
    out = refs[-1]
    span, state = c_input.shape
    wide = wide_row.shape[1] // GROUP
    heads = wide_row.shape[1] // HEAD_DIM
    queries = jnp.concatenate([c_input[...]] * 2, axis=1)
    by_token = columns[:, 128:]
    squares = jnp.zeros((span, 128), jnp.float32)
    values = jnp.zeros((span, 128), jnp.float32)
    for slot, piece in zip(slots, entering):
        part = partner_index(orders, slot)
        lanes = pl.ds(pl.multiple_of(part * wide, wide), wide)
        value = jnp.concatenate([piece[:state, :], piece[state:, :]], axis=1)
        high = value.astype(jnp.bfloat16)
        low = (value - high.astype(jnp.float32)).astype(jnp.bfloat16)
        carried = dot(queries, jnp.concatenate([high, low], axis=0))
        decay = dot(by_token, selector(heads, 128, part * (heads // GROUP), wide))
        mixed = inside[:, lanes] + carried * decay
        readout = wide_row[0:1, lanes]
        squared, read = mixed * mixed, mixed * readout
        for k in range(0, wide, 128):
            squares = squares + squared[:, k : k + 128]
            values = values + read[:, k : k + 128]
    squares = jnp.sum(squares.T, axis=0, keepdims=True)
    values = jnp.sum(values.T, axis=0, keepdims=True)
    if len(refs) > 1:
        squares, values = squares + refs[0][0:1, :], values + refs[0][1:2, :]
    out[0:1, :] = squares
    out[1:2, :] = values


def last_kernel(channels, first_group_early, mine, other, suffix, carry, got, values_out, advantages_out, values, advantages, sems):
    sums = mine[...] + other[...]
    value = sums[1:2] / jnp.sqrt(sums[0:1] / channels + NORM_EPSILON)
    values[...] = value
    amount = carry[0:1, 0:1]
    if first_group_early:
        later = jnp.where(lax.axis_index("ctx") < GROUP, got[0:1, 0:1], 0.0)
        amount = amount + carry[1:2, 0:1] * later
    advantages[...] = suffix[0:1, :] + suffix[1:2, :] * amount - value
    copies = [
        pltpu.make_async_copy(values, values_out, sems.at[0]),
        pltpu.make_async_copy(advantages, advantages_out, sems.at[1]),
    ]
    for copy in copies:
        copy.start()
    for copy in copies:
        copy.wait()


def call(kernel, shapes, name, *args, hbm_in=False, hbm_out=False, scratch=(), aliases=None):
    near, far = pl.BlockSpec(memory_space=pltpu.VMEM), pl.BlockSpec(memory_space=pltpu.HBM)
    if hbm_in:
        args = [pltpu.with_memory_space_constraint(arg, pltpu.HBM) for arg in args]
    return pl.pallas_call(
        kernel,
        out_shape=[jax.ShapeDtypeStruct(*shape) for shape in shapes],
        in_specs=[far if hbm_in else near] * len(args),
        out_specs=[far if hbm_out else near] * len(shapes),
        scratch_shapes=scratch,
        input_output_aliases=aliases or {},
        compiler_params=pltpu.CompilerParams(vmem_limit_bytes=VMEM_BYTES),
        name=name,
    )(*args)


def swap(value, axis, mask):
    count = lax.axis_size(axis)
    return lax.ppermute(value, axis, [(k, k ^ mask) for k in range(count)])


def swap_slots(orders, pieces):
    cores = lax.axis_size("head")
    assert cores == len(orders)
    pairs = [
        [
            (k * cores + core, (k ^ orders[core][slot]) * cores + core)
            for k in range(lax.axis_size("ctx"))
            for core in range(cores)
        ]
        for slot in range(1, GROUP)
    ]
    return [lax.ppermute(piece, ("ctx", "head"), pair) for piece, pair in zip(pieces, pairs)]


def local(
    features,
    b_input,
    c_input,
    step_input,
    decay_log,
    skip_gain,
    norm_gain,
    value_weight,
    rewards,
    reward_keep_mask,
    episode_end,
):
    span, width = features.shape
    heads = step_input.shape[0]
    state = b_input.shape[1]
    halves = width // GROUP // LANES
    count = lax.axis_size("ctx")
    groups = count // GROUP
    assert span == SPAN and count == groups * GROUP and groups > 1 and groups & (groups - 1) == 0 and halves == 2
    f32, bf16, i32 = jnp.float32, jnp.bfloat16, jnp.int32
    piece = ((halves * state + EXTRA, LANES), f32)
    states = ((halves * state, LANES), f32)
    columns_shape, wide_shape, inside_shape = ((span, 256), bf16), ((2, width), f32), ((span, width), f32)

    made = call(
        state_kernel,
        [piece] * (GROUP - 1)
        + [
            ((span, width), bf16),
            ((span, state), bf16),
            ((span, state), bf16),
            ((heads, span), f32),
            ((heads, span), f32),
            ((8, span), f32),
            ((1, heads), f32),
            ((1, width), f32),
            ((1, width), f32),
            ((span, 128), f32),
            columns_shape,
            wide_shape,
            inside_shape,
        ],
        "block_states",
        step_input,
        decay_log[None, :],
        rewards[None, :],
        reward_keep_mask[None, :],
        episode_end[None, :],
        features,
        b_input,
        c_input,
        skip_gain[None, :],
        norm_gain[None, :],
        value_weight[None, :],
        hbm_in=True,
        scratch=[
            pltpu.VMEM((heads, span), f32),
            pltpu.VMEM((1, heads), f32),
            pltpu.VMEM((1, span), f32),
            pltpu.VMEM((1, span), i32),
            pltpu.VMEM((1, span), i32),
            pltpu.SemaphoreType.DMA((11,)),
        ],
    )
    pieces, made = made[: GROUP - 1], made[GROUP - 1 :]
    moved = swap_slots(FIRST_ORDERS, pieces)
    columns, wide_row, inside, suffix, own_piece = call(
        first_kernel,
        [columns_shape, wide_shape, inside_shape, ((8, span), f32), piece],
        "inside_first",
        *made,
        aliases={10: 0, 11: 1, 12: 2},
    )
    got = [own_piece, *moved]
    near = (*made[:5], columns, wide_row)
    queries = made[2]
    (total,) = call(
        functools.partial(total_kernel, groups == 2),
        [states if groups == 2 else piece],
        "group_total",
        *got,
        suffix,
    )
    past = None
    bit = 1
    while bit * 2 < groups:
        other = swap(total, "ctx", GROUP * bit)
        if past is None:
            row = jnp.arange(piece[0][0])[:, None]
            past = jnp.where(row == halves * (state + 1), 1.0, 0.0).astype(f32) * jnp.ones((1, LANES), f32)
        total, past = call(
            functools.partial(round_kernel, bit), [piece, piece], "scan_round", total, other, past
        )
        bit *= 2
    other = swap(total, "ctx", GROUP * bit)
    (inside,) = call(second_kernel, [inside_shape], "inside_second", *near, inside, aliases={len(near): 0})

    def finish(has_got):
        orders = LAST_ORDERS if has_got else EARLY_ORDERS
        operands = (*got, *([other] if has_got else []), *([] if past is None else [past]))
        made = call(
            functools.partial(entering_kernel, bit, orders, has_got, past is not None),
            [states] * GROUP + [((8, LANES), f32)],
            "entering_states",
            *operands,
            *([] if past is None else [inside]),
        )
        arrived = [made[0], *swap_slots(orders, made[1:GROUP])]
        sums = ()
        for slots in READOUTS:
            sums = call(
                functools.partial(readout_kernel, orders, slots),
                [((2, span), f32)],
                "readout",
                *(arrived[slot] for slot in slots),
                queries,
                columns,
                inside,
                wide_row,
                *sums,
            )
        return sums[0], made[GROUP]

    first_group_early = groups == 2
    if first_group_early:
        is_first = lax.axis_index("ctx") < GROUP
        nothing = lambda: (jnp.zeros((2, span), f32), jnp.zeros((8, LANES), f32))
        early = lax.cond(is_first, lambda: finish(False), nothing)
        sums, carry = lax.cond(is_first, lambda: early, lambda: finish(True))
    else:
        sums, carry = finish(True)
    values, advantages = call(
        functools.partial(last_kernel, width * lax.axis_size("head"), first_group_early),
        [((1, span), f32)] * 2,
        "values_and_advantages",
        sums,
        swap(sums, "head", 1),
        suffix,
        carry,
        other,
        hbm_out=True,
        scratch=[pltpu.VMEM((1, span), f32), pltpu.VMEM((1, span), f32), pltpu.SemaphoreType.DMA((2,))],
    )
    return (values[0], advantages[0])


def solution(mesh):
    placed = (
        P(("traj", "ctx"), "head"),
        P(("traj", "ctx"), None),
        P(("traj", "ctx"), None),
        P("head", ("traj", "ctx")),
        P("head"),
        P("head"),
        P("head"),
        P("head"),
        P(("traj", "ctx")),
        P(("traj", "ctx")),
        P(("traj", "ctx")),
    )
    return jax.shard_map(
        local,
        mesh=mesh,
        in_specs=placed,
        out_specs=(P(("traj", "ctx")), P(("traj", "ctx"))),
        check_vma=False,
    )
```

```python
import functools

import jax
import jax.numpy as jnp
from jax import lax
from jax.experimental import pallas as pl
from jax.experimental.pallas import tpu as pltpu
from jax.sharding import PartitionSpec as P

HEAD_DIM = 32
SPAN = 256
GROUP = 4
LANES = 128
FIRST_ORDERS = ((0, 1, 2, 3), (0, 2, 1, 3))
EARLY_ORDERS = ((0, 3, 1, 2), (0, 1, 2, 3))
LAST_ORDERS = ((0, 3, 1, 2), (0, 1, 2, 3))
READOUTS = ((0, 1, 2, 3),)
SHARES = (((0, 1, 4, 8), (0, 0, 7, 8)), ((0, 1, 6, 8), (0, 0, 6, 8)))
EXTRA = 8
NORM_EPSILON = 1e-05
VMEM_BYTES = 24 * 1024 * 1024


def split3(value):
    high = value.astype(jnp.bfloat16).astype(jnp.float32)
    rest = value - high
    middle = rest.astype(jnp.bfloat16).astype(jnp.float32)
    return high, middle, (rest - middle).astype(jnp.bfloat16).astype(jnp.float32)


def dot(a, b, contract=((1,), (0,))):
    return lax.dot_general(a, b, (contract, ((), ())), preferred_element_type=jnp.float32)


def iota(shape, dim):
    return lax.broadcasted_iota(jnp.int32, shape, dim)


def column(row):
    n = row.shape[1]
    return jnp.sum(jnp.where(iota((n, n), 0) == iota((n, n), 1), row, 0.0), axis=1, keepdims=True)


def over_channels(per_head, first_head, channels):
    heads = per_head.shape[0]
    match = iota((heads, channels), 0) == first_head + iota((heads, channels), 1) // HEAD_DIM
    return jnp.sum(jnp.where(match, per_head, 0.0), axis=0, keepdims=True)


def selector(heads, rows, first_head, channels):
    row = iota((rows, channels), 0)
    match = (lax.rem(row, heads) == first_head + iota((rows, channels), 1) // HEAD_DIM) & (row < 3 * heads)
    return jnp.where(match, 1.0, 0.0).astype(jnp.bfloat16)


def member_index():
    return lax.rem(lax.axis_index("ctx"), GROUP)


def partner_index(orders, slot):
    return lax.bitwise_xor(member_index(), jnp.where(lax.axis_index("head") == 0, orders[0][slot], orders[1][slot]))


def each_place(last_orders, body):
    for core in range(len(FIRST_ORDERS)):
        for v in range(GROUP):

            @pl.when((member_index() == v) & (lax.axis_index("head") == core))
            def _():
                body(v, *([orders[core].index(v ^ m) for m in range(GROUP)] for orders in (FIRST_ORDERS, last_orders)))


def prepare(cum_ref, skip, norm, weight, columns_out, wide_out):
    heads, span = cum_ref.shape
    cum = cum_ref[...]
    pad = jnp.zeros((128 - 3 * heads, span), jnp.float32)
    columns_out[:, :128] = jnp.concatenate(split3(cum) + (jnp.ones_like(pad),), axis=0).T.astype(jnp.bfloat16)
    columns_out[:, 128:] = jnp.concatenate(split3(jnp.exp(cum)) + (pad,), axis=0).T.astype(jnp.bfloat16)
    wide_out[0:1, :] = norm[...] * weight[...]
    wide_out[1:2, :] = over_channels(column(skip[...]), 0, heads * HEAD_DIM)


def write_pieces(slots, token, features, b_input, total, still_open, first_sum, outs):
    keys = b_input[...].T
    state = keys.shape[0]
    heads = total.shape[0]
    wide = features.shape[1] // GROUP
    row = iota((EXTRA, LANES), 0)
    by_token = token[...].astype(jnp.bfloat16)
    places = [partner_index(FIRST_ORDERS, slot) for slot in slots]
    spread = [dot(by_token, selector(heads, 128, part * (heads // GROUP), wide)) for part in places]
    feats = [features[:, pl.ds(pl.multiple_of(part * wide, wide), wide)] for part in places]
    scaled = [(one * feat.astype(jnp.float32)).astype(jnp.bfloat16) for one, feat in zip(spread, feats)]
    states = [dot(keys, one) for one in scaled]
    for part, one, out in zip(places, states, outs):
        decay = over_channels(total, part * (heads // GROUP), wide)
        extra = jnp.where(row == wide // LANES, still_open, first_sum)
        for k in range(wide // LANES):
            out[k * state : (k + 1) * state, :] = one[:, k * LANES : (k + 1) * LANES]
            extra = jnp.where(row == k, decay[:, k * LANES : (k + 1) * LANES], extra)
        out[wide // LANES * state :, :] = extra


def state_kernel(*refs):
    sources, refs = refs[:11], refs[11:]
    pieces, refs = refs[: GROUP - 1], refs[GROUP - 1 :]
    features, b_input, c_input, cum_out, step_out, rows, skip, norm, weight, token, columns, wide_row, inside = refs[:13]
    step_in, decay_log, rewards, keep, ends, sems = refs[13:]
    targets = (step_in, decay_log, rewards, keep, ends, features, b_input, c_input, skip, norm, weight)
    copies = [pltpu.make_async_copy(src, dst, sems.at[i]) for i, (src, dst) in enumerate(zip(sources, targets))]
    for copy in copies:
        copy.start()
    heads, span = step_in.shape
    for copy in copies[:5]:
        copy.wait()
    raw = step_in[...]
    step = jnp.maximum(raw, 0.0) + jnp.log1p(jnp.exp(-jnp.abs(raw)))
    log_decay = -jnp.exp(column(decay_log[...])) * step
    ends_row = ends[...].astype(jnp.float32)
    live = keep[...].astype(jnp.float32) * rewards[...]
    upper = jnp.where(iota((span, span), 0) <= iota((span, span), 1), 1.0, 0.0).astype(jnp.bfloat16)
    stacked = jnp.concatenate(split3(log_decay) + (jnp.broadcast_to(ends_row, (16, span)),), axis=0)
    summed = dot(stacked.astype(jnp.bfloat16), upper)
    cum = summed[:heads] + summed[heads : 2 * heads] + summed[2 * heads : 3 * heads]
    through = summed[3 * heads : 3 * heads + 1]
    before = through - ends_row
    total = cum[:, span - 1 :]
    first_sum = jnp.sum(jnp.where(before == 0.0, live, 0.0), axis=1, keepdims=True)
    still_open = jnp.where(through[:, span - 1 :] == 0.0, 1.0, 0.0)
    coefficient = jnp.exp(total - cum) * step
    pad = jnp.zeros((128 - 3 * heads, span), jnp.float32)
    token[...] = jnp.concatenate(split3(coefficient) + (pad,), axis=0).T
    cum_out[...] = cum
    step_out[...] = step
    flags = [jnp.broadcast_to(value, (1, span)) for value in (still_open, first_sum)]
    rows[...] = jnp.concatenate([live, through, before, *flags, jnp.zeros((3, span), jnp.float32)], axis=0)
    for copy in copies[5:]:
        copy.wait()

    @pl.when(share_bound(1) > 0)
    def _():
        prepare(cum_out, skip, norm, weight, columns, wide_row)
        intra_groups(0, features, b_input, c_input, cum_out, step_out, columns, wide_row, inside)

    write_pieces((1, 2, 3), token, features, b_input, total, still_open, first_sum, pieces)


def share_bound(k):
    first_group, first_core = lax.axis_index("ctx") < GROUP, lax.axis_index("head") == 0
    return jnp.where(
        first_group,
        jnp.where(first_core, SHARES[0][0][k], SHARES[0][1][k]),
        jnp.where(first_core, SHARES[1][0][k], SHARES[1][1][k]),
    )


def intra_groups(stage, features, b_input, c_input, cum_ref, step_ref, columns, wide_row, out):
    start, stop = share_bound(stage), share_bound(stage + 1)
    heads, span = cum_ref.shape
    at_once = 128 // HEAD_DIM
    t, s = iota((span, span), 0), iota((span, span), 1)
    scores = jnp.where(t >= s, dot(c_input[...], b_input[...], ((1,), (1,))), 0.0)
    by_token = columns[:, :128]
    row = iota((128, span), 0)

    def some_heads(index, carry):
        first = index * at_once
        lanes = pl.ds(pl.multiple_of(index * 128, 128), 128)
        feat = features[:, lanes]
        total = feat.astype(jnp.float32) * wide_row[1:2, lanes]
        owner = iota((span, 128), 1) // HEAD_DIM
        gaps = []
        for head in (first + j for j in range(at_once)):
            high, middle, low = split3(cum_ref[pl.ds(head, 1), :])
            other = jnp.where(
                row < 3 * heads,
                jnp.where(lax.rem(row, heads) == head, 1.0, 0.0),
                jnp.where(
                    row == 3 * heads,
                    -high,
                    jnp.where(row == 3 * heads + 1, -middle, jnp.where(row == 3 * heads + 2, -low, 0.0)),
                ),
            ).astype(jnp.bfloat16)
            gaps.append(jnp.minimum(dot(by_token, other), 0.0))
        weights = [
            (scores * jnp.exp(gap) * step_ref[pl.ds(first + j, 1), :]).astype(jnp.bfloat16)
            for j, gap in enumerate(gaps)
        ]
        for j, weight in enumerate(weights):
            total = total + dot(weight, jnp.where(owner == j, feat, jnp.zeros_like(feat)))
        out[:, lanes] = total
        return carry

    lax.fori_loop(start, stop, some_heads, 0)


def first_kernel(
    features,
    b_input,
    c_input,
    cum_ref,
    step_ref,
    rows,
    skip,
    norm,
    weight,
    token,
    _0,
    _1,
    _2,
    columns,
    wide_row,
    out,
    suffix,
    own_piece,
):
    span = cum_ref.shape[1]
    write_pieces(
        (0,), token, features, b_input, cum_ref[:, span - 1 :], rows[3:4, 0:1], rows[4:5, 0:1], (own_piece,)
    )

    @pl.when(share_bound(1) == 0)
    def _():
        prepare(cum_ref, skip, norm, weight, columns, wide_row)

    intra_groups(1, features, b_input, c_input, cum_ref, step_ref, columns, wide_row, out)

    t, s = iota((span, span), 0), iota((span, span), 1)
    live, through, before = rows[0:1, :], rows[1:2, :], rows[2:3, :]
    reach = jnp.where((t >= s) & (column(before) == before), column(live), 0.0)
    sums = jnp.sum(reach, axis=0, keepdims=True)
    open_end = jnp.where(before == through[:, span - 1 :], 1.0, 0.0)
    suffix[...] = jnp.concatenate([sums, open_end, jnp.zeros((6, span), jnp.float32)], axis=0)


def second_kernel(features, b_input, c_input, cum_ref, step_ref, columns, wide_row, _, out):
    intra_groups(2, features, b_input, c_input, cum_ref, step_ref, columns, wide_row, out)


def parts_of(piece):
    halves = 2
    size = (piece.shape[0] - EXTRA) // halves
    extra = piece[halves * size :, :]
    return (
        [piece[k * size : (k + 1) * size, :] for k in range(halves)],
        [extra[k : k + 1] for k in range(halves)],
        extra[halves : halves + 1],
        extra[halves + 1 : halves + 2],
    )


def write_piece(out, states, decays, keeps, amount):
    size = states[0].shape[0]
    for k, state in enumerate(states):
        out[k * size : (k + 1) * size, :] = state
    row = iota((EXTRA, LANES), 0)
    extra = jnp.where(row == len(states), keeps, amount)
    for k, decay in enumerate(decays):
        extra = jnp.where(row == k, decay, extra)
    out[len(states) * size :, :] = extra


def carry_on(states, piece):
    return [jnp.exp(decay) * old + new for old, new, decay in zip(states, piece[0], piece[1])]


def add(first, second):
    return [one + other for one, other in zip(first, second)]


def total_kernel(two_groups, *refs):
    pieces, out = refs[:GROUP], refs[-1]

    @functools.partial(each_place, FIRST_ORDERS)
    def _(me, first, last):
        members = [parts_of(pieces[slot]) for slot in first]
        states, decays, keeps, _ = members[0]
        for member in members[1:]:
            states = carry_on(states, member)
            decays = add(decays, member[1])
            keeps = keeps * member[2]
        amount = members[-1][3]
        for member in members[-2::-1]:
            amount = member[3] + member[2] * amount
        if not two_groups:
            write_piece(out, states, decays, keeps, amount)
            return

        @pl.when(lax.axis_index("ctx") < GROUP)
        def _():
            for k, state in enumerate(states):
                out[k * state.shape[0] : (k + 1) * state.shape[0], :] = state

        @pl.when(lax.axis_index("ctx") >= GROUP)
        def _():
            out[:EXTRA, :] = jnp.broadcast_to(amount, (EXTRA, LANES))


def round_kernel(bit, *refs):
    total, got, before, total_out, before_out = refs
    group = lax.axis_index("ctx") // GROUP
    mine, theirs, past = parts_of(total), parts_of(got), parts_of(before)
    decays, keeps = add(mine[1], theirs[1]), mine[2] * theirs[2]

    @pl.when(lax.rem(group // bit, 2) == 1)
    def _():
        write_piece(before_out, carry_on(theirs[0], past), add(past[1], theirs[1]), past[2], past[3])
        write_piece(total_out, carry_on(theirs[0], mine), decays, keeps, theirs[3] + theirs[2] * mine[3])

    @pl.when(lax.rem(group // bit, 2) == 0)
    def _():
        write_piece(before_out, past[0], past[1], past[2] * theirs[2], past[3] + past[2] * theirs[3])
        write_piece(total_out, carry_on(mine[0], theirs), decays, keeps, mine[3] + mine[2] * theirs[3])


def entering_kernel(bit, orders, has_got, has_past, *refs):
    pieces, refs = refs[:GROUP], refs[GROUP:]
    got, refs = (refs[0], refs[1:]) if has_got else (None, refs)
    past, refs = (refs[0], refs[1:]) if has_past else (None, refs)
    outs, carry_out = refs[-GROUP - 1 : -1], refs[-1]
    is_later = lax.rem(lax.axis_index("ctx") // GROUP // bit, 2) == 1

    @functools.partial(each_place, orders)
    def _(me, first, last):
        members = [parts_of(pieces[slot]) for slot in first]
        size = members[0][0][0].shape
        arriving = [jnp.zeros(size, jnp.float32)] * 2
        keeps, amount = jnp.ones((1, LANES), jnp.float32), jnp.zeros((1, LANES), jnp.float32)
        if has_got and got.shape[0] == 2 * size[0]:
            arriving = [got[: size[0], :], got[size[0] :, :]]
        elif has_got:
            theirs = parts_of(got)
            arriving = [jnp.where(is_later, state, 0.0) for state in theirs[0]]
            keeps = jnp.where(is_later, keeps, theirs[2])
            amount = jnp.where(is_later, amount, theirs[3])
        if has_past:
            old = parts_of(past)
            arriving = carry_on(arriving, old)
            amount = old[3] + old[2] * amount
        for m in range(GROUP):
            for k, state in enumerate(arriving):
                outs[last[m]][k * size[0] : (k + 1) * size[0], :] = state
            if m < GROUP - 1:
                arriving = carry_on(arriving, members[m])
        for m in range(GROUP - 1, me, -1):
            amount = members[m][3] + members[m][2] * amount
            keeps = keeps * members[m][2]
        row = iota(carry_out.shape, 0)
        carry_out[...] = jnp.where(row == 0, amount, keeps)


def readout_kernel(orders, slots, *refs):
    entering, (c_input, columns, inside, wide_row), refs = refs[: len(slots)], refs[len(slots) :][:4], refs[len(slots) + 4 :]
    out = refs[-1]
    span, state = c_input.shape
    wide = wide_row.shape[1] // GROUP
    heads = wide_row.shape[1] // HEAD_DIM
    queries = jnp.concatenate([c_input[...]] * 2, axis=1)
    by_token = columns[:, 128:]
    squares = jnp.zeros((span, 128), jnp.float32)
    values = jnp.zeros((span, 128), jnp.float32)
    for slot, piece in zip(slots, entering):
        part = partner_index(orders, slot)
        lanes = pl.ds(pl.multiple_of(part * wide, wide), wide)
        value = jnp.concatenate([piece[:state, :], piece[state:, :]], axis=1)
        high = value.astype(jnp.bfloat16)
        low = (value - high.astype(jnp.float32)).astype(jnp.bfloat16)
        carried = dot(queries, jnp.concatenate([high, low], axis=0))
        decay = dot(by_token, selector(heads, 128, part * (heads // GROUP), wide))
        mixed = inside[:, lanes] + carried * decay
        readout = wide_row[0:1, lanes]
        squared, read = mixed * mixed, mixed * readout
        for k in range(0, wide, 128):
            squares = squares + squared[:, k : k + 128]
            values = values + read[:, k : k + 128]
    squares = jnp.sum(squares.T, axis=0, keepdims=True)
    values = jnp.sum(values.T, axis=0, keepdims=True)
    if len(refs) > 1:
        squares, values = squares + refs[0][0:1, :], values + refs[0][1:2, :]
    out[0:1, :] = squares
    out[1:2, :] = values


def last_kernel(channels, first_group_early, mine, other, suffix, carry, got, values_out, advantages_out, values, advantages, sems):
    sums = mine[...] + other[...]
    value = sums[1:2] / jnp.sqrt(sums[0:1] / channels + NORM_EPSILON)
    values[...] = value
    amount = carry[0:1, 0:1]
    if first_group_early:
        later = jnp.where(lax.axis_index("ctx") < GROUP, got[0:1, 0:1], 0.0)
        amount = amount + carry[1:2, 0:1] * later
    advantages[...] = suffix[0:1, :] + suffix[1:2, :] * amount - value
    copies = [
        pltpu.make_async_copy(values, values_out, sems.at[0]),
        pltpu.make_async_copy(advantages, advantages_out, sems.at[1]),
    ]
    for copy in copies:
        copy.start()
    for copy in copies:
        copy.wait()


def call(kernel, shapes, name, *args, hbm_in=False, hbm_out=False, scratch=(), aliases=None):
    near, far = pl.BlockSpec(memory_space=pltpu.VMEM), pl.BlockSpec(memory_space=pltpu.HBM)
    if hbm_in:
        args = [pltpu.with_memory_space_constraint(arg, pltpu.HBM) for arg in args]
    return pl.pallas_call(
        kernel,
        out_shape=[jax.ShapeDtypeStruct(*shape) for shape in shapes],
        in_specs=[far if hbm_in else near] * len(args),
        out_specs=[far if hbm_out else near] * len(shapes),
        scratch_shapes=scratch,
        input_output_aliases=aliases or {},
        compiler_params=pltpu.CompilerParams(vmem_limit_bytes=VMEM_BYTES),
        name=name,
    )(*args)


def swap(value, axis, mask):
    count = lax.axis_size(axis)
    return lax.ppermute(value, axis, [(k, k ^ mask) for k in range(count)])


def swap_slots(orders, pieces):
    cores = lax.axis_size("head")
    assert cores == len(orders)
    pairs = [
        [
            (k * cores + core, (k ^ orders[core][slot]) * cores + core)
            for k in range(lax.axis_size("ctx"))
            for core in range(cores)
        ]
        for slot in range(1, GROUP)
    ]
    return [lax.ppermute(piece, ("ctx", "head"), pair) for piece, pair in zip(pieces, pairs)]


def local(
    features,
    b_input,
    c_input,
    step_input,
    decay_log,
    skip_gain,
    norm_gain,
    value_weight,
    rewards,
    reward_keep_mask,
    episode_end,
):
    span, width = features.shape
    heads = step_input.shape[0]
    state = b_input.shape[1]
    halves = width // GROUP // LANES
    count = lax.axis_size("ctx")
    groups = count // GROUP
    assert span == SPAN and count == groups * GROUP and groups > 1 and groups & (groups - 1) == 0 and halves == 2
    f32, bf16, i32 = jnp.float32, jnp.bfloat16, jnp.int32
    piece = ((halves * state + EXTRA, LANES), f32)
    states = ((halves * state, LANES), f32)
    columns_shape, wide_shape, inside_shape = ((span, 256), bf16), ((2, width), f32), ((span, width), f32)

    made = call(
        state_kernel,
        [piece] * (GROUP - 1)
        + [
            ((span, width), bf16),
            ((span, state), bf16),
            ((span, state), bf16),
            ((heads, span), f32),
            ((heads, span), f32),
            ((8, span), f32),
            ((1, heads), f32),
            ((1, width), f32),
            ((1, width), f32),
            ((span, 128), f32),
            columns_shape,
            wide_shape,
            inside_shape,
        ],
        "block_states",
        step_input,
        decay_log[None, :],
        rewards[None, :],
        reward_keep_mask[None, :],
        episode_end[None, :],
        features,
        b_input,
        c_input,
        skip_gain[None, :],
        norm_gain[None, :],
        value_weight[None, :],
        hbm_in=True,
        scratch=[
            pltpu.VMEM((heads, span), f32),
            pltpu.VMEM((1, heads), f32),
            pltpu.VMEM((1, span), f32),
            pltpu.VMEM((1, span), i32),
            pltpu.VMEM((1, span), i32),
            pltpu.SemaphoreType.DMA((11,)),
        ],
    )
    pieces, made = made[: GROUP - 1], made[GROUP - 1 :]
    moved = swap_slots(FIRST_ORDERS, pieces)
    columns, wide_row, inside, suffix, own_piece = call(
        first_kernel,
        [columns_shape, wide_shape, inside_shape, ((8, span), f32), piece],
        "inside_first",
        *made,
        aliases={10: 0, 11: 1, 12: 2},
    )
    got = [own_piece, *moved]
    near = (*made[:5], columns, wide_row)
    queries = made[2]
    (total,) = call(
        functools.partial(total_kernel, groups == 2),
        [states if groups == 2 else piece],
        "group_total",
        *got,
        suffix,
    )
    past = None
    bit = 1
    while bit * 2 < groups:
        other = swap(total, "ctx", GROUP * bit)
        if past is None:
            row = jnp.arange(piece[0][0])[:, None]
            past = jnp.where(row == halves * (state + 1), 1.0, 0.0).astype(f32) * jnp.ones((1, LANES), f32)
        total, past = call(
            functools.partial(round_kernel, bit), [piece, piece], "scan_round", total, other, past
        )
        bit *= 2
    other = swap(total, "ctx", GROUP * bit)
    (inside,) = call(second_kernel, [inside_shape], "inside_second", *near, inside, aliases={len(near): 0})

    def finish(has_got):
        orders = LAST_ORDERS if has_got else EARLY_ORDERS
        operands = (*got, *([other] if has_got else []), *([] if past is None else [past]))
        made = call(
            functools.partial(entering_kernel, bit, orders, has_got, past is not None),
            [states] * GROUP + [((8, LANES), f32)],
            "entering_states",
            *operands,
            *([] if past is None else [inside]),
        )
        arrived = [made[0], *swap_slots(orders, made[1:GROUP])]
        sums = ()
        for slots in READOUTS:
            sums = call(
                functools.partial(readout_kernel, orders, slots),
                [((2, span), f32)],
                "readout",
                *(arrived[slot] for slot in slots),
                queries,
                columns,
                inside,
                wide_row,
                *sums,
            )
        return sums[0], made[GROUP]

    first_group_early = groups == 2
    if first_group_early:
        is_first = lax.axis_index("ctx") < GROUP
        nothing = lambda: (jnp.zeros((2, span), f32), jnp.zeros((8, LANES), f32))
        early = lax.cond(is_first, lambda: finish(False), nothing)
        sums, carry = lax.cond(is_first, lambda: early, lambda: finish(True))
    else:
        sums, carry = finish(True)
    values, advantages = call(
        functools.partial(last_kernel, width * lax.axis_size("head"), first_group_early),
        [((1, span), f32)] * 2,
        "values_and_advantages",
        sums,
        swap(sums, "head", 1),
        suffix,
        carry,
        other,
        hbm_out=True,
        scratch=[pltpu.VMEM((1, span), f32), pltpu.VMEM((1, span), f32), pltpu.SemaphoreType.DMA((2,))],
    )
    return (values[0], advantages[0])


def solution(mesh):
    placed = (
        P(("traj", "ctx"), "head"),
        P(("traj", "ctx"), None),
        P(("traj", "ctx"), None),
        P("head", ("traj", "ctx")),
        P("head"),
        P("head"),
        P("head"),
        P("head"),
        P(("traj", "ctx")),
        P(("traj", "ctx")),
        P(("traj", "ctx")),
    )
    return jax.shard_map(
        local,
        mesh=mesh,
        in_specs=placed,
        out_specs=(P(("traj", "ctx")), P(("traj", "ctx"))),
        check_vma=False,
    )
```
